32 devices in a mesh: member: 2 (over x), lon: 16 (over z, y, core).
Axes of the slice: x: 2, y: 2, z: 4, core: 2. Of those that a mesh axis runs over, the one named last changes fastest.
Arguments:
- obs_owner: int32 [4096, 2], P('lon', 'member'), parts along dimension 1, may hold values from 0 to 15; in each aligned block of 256 rows (0 to 255, 256 to 511, ...) at most 32 rows name the same one
- obs_lonpos: int32 [8192], P(('member', 'lon')), parts along dimension 0, may hold values from 0 to 7
- obs_lat: int32 [8192], P(('member', 'lon')), parts along dimension 0, may hold values from 0 to 127
- obs_step: int32 [8192], P(('member', 'lon')), parts along dimension 0, may hold values from 1 to 3
- obs_top: int32 [8192], P(('member', 'lon')), parts along dimension 0, may hold values from 1 to 128
- innovation: float32 [256, 4096], P('member', 'lon'), parts along dimension 0, may hold values from -6 to 6
- obs_weight: float32 [256, 4096], P('member', 'lon'), parts along dimension 0, may hold values from 0.2 to 2
- wind_shift: int32 [3, 128, 128], replicated, may hold values from -1 to 1
- wind_frac: float32 [3, 128, 128], replicated, may hold values from 0 to 1
- vmix: float32 [4, 128, 128], replicated, may hold values from -0.5 to 1
- hcoef: float32 [4, 128], replicated, may hold values from -3 to 3
Outputs:
- increment: float32 [8, 128, 128, 128], P('member', None, 'lon'), parts along dimension 0
- residual: float32 [8, 128, 128, 128], P('member', None, 'lon'), parts along dimension 0
The draws below stay inside these ranges and needn't reach their ends.
There are 2 independent parts, one for each index of `member`. The reference program is written for one: setup_inputs(seed, part) draws one part's arguments, and reference() takes and returns one part's arrays. A program takes and returns all parts, laid end to end along the dimension named above; an argument that names none is the same for every part. Nothing has to cross between parts.
Inputs may be any that keep to these rules, and one draw needn't show every extreme that they name: `obs_owner`: in the rows of one device at most 32 profiles name the same band, and some device's rows reach 32 for some band.
All inputs are finite; a program needn't handle non-finite values.
Results may differ from the reference program's by a relative error of at most 0.0003.
Values sent between devices are 32-bit elements; how exact they have to be, the bound alone decides.
No kernel may reach another device: no remote copies, remote signals or barrier semaphores. Data moves between devices by JAX's collectives and lax.ppermute only.
A program may use at most 64 MiB of HBM per device.

```python
import math
import jax
import jax.numpy as jnp
import numpy as np
from jax import lax

FIELDS = 4
L = 128
LON_DEV = 8
NLAT = 128
OBS_DEV = 256
NSTEP = 3
ITERS = 2
NLON = 128
NOBS = 4096
CAP = 32
N_LON = 16


def draw_vmix(key, part):
    key = jax.random.fold_in(key, 11)
    identity = jnp.eye(L, dtype=jnp.float32)
    noise = jax.random.normal(key, (FIELDS, L, L), jnp.float32) * (0.35 / L ** 0.5)
    return 0.55 * identity[None, :, :] + noise


def touch_ends(values, stream_key, smallest, largest):
    index_at = [jax.random.randint(jax.random.fold_in(stream_key, axis), (), 0, length) for axis, length in enumerate(values.shape)]
    widest = values.shape.index(max(values.shape))
    neighbour = index_at[:widest] + [(index_at[widest] + 1) % values.shape[widest]] + index_at[widest + 1:]
    return values.at[tuple(index_at)].set(smallest).at[tuple(neighbour)].set(largest)


def steps_of(key, dims, shards, smallest, largest):
    factor_of, own = 1.0, jax.random.fold_in(key, 6)
    for axis_at, blocks in shards:
        draws = jnp.exp(jax.random.uniform(jax.random.fold_in(own, axis_at), (blocks,), jnp.float32, smallest / len(shards), largest / len(shards)))
        factor_of = factor_of * jnp.repeat(draws, dims[axis_at] // blocks).reshape([-1 if axis == axis_at else 1 for axis in range(len(dims))])
    return factor_of


def shared_out(own_key, own, number, rows, amount, top, bound, slope):
    order = jax.random.permutation(own_key, amount)
    heavy_load, usual = shares(amount, rows * top, bound, slope, True), shares(amount, rows * top, bound, slope, False)
    places = jnp.arange(amount)

    def named(sizes, offset_by):
        used = int((sizes > 0).sum())
        fixed = max(1, used // 4)
        passed = fixed + (places - fixed + offset_by * (used - fixed)) % max(1, amount - fixed)
        return jnp.zeros((amount,), jnp.int32).at[order[jnp.where(places < fixed, places, passed)]].set(jnp.asarray(sizes, jnp.int32))

    sizes = jnp.where(number % 4 == 0, named(heavy_load, number // 4), named(usual, number - number // 4 - 1))
    mixed = jax.random.permutation(jax.random.fold_in(own, 3), amount)
    donor, taker = mixed[0:amount // 2 * 2:2], mixed[1:amount // 2 * 2:2]
    room = jnp.minimum(sizes[donor] - 1, bound - sizes[taker]) // 2
    room = jnp.where((donor == order[0]) | (taker == order[0]) | (sizes[taker] == 0), 0, jnp.maximum(room, 0))
    passed = jax.random.randint(jax.random.fold_in(own, 4), (amount // 2,), 0, 1 << 20) % (room + 1)
    sizes = sizes.at[donor].add(-passed).at[taker].add(passed)
    members = jnp.searchsorted(jnp.cumsum(sizes), jnp.arange(rows * top), side="right").astype(jnp.int32)
    table = members.reshape(top, rows).T
    table = table[jax.random.permutation(jax.random.fold_in(own, 1), rows)]
    offset_by = jax.random.randint(jax.random.fold_in(own, 2), (rows, 1), 0, top)
    return jnp.take_along_axis(table, (jnp.arange(top)[None, :] + offset_by) % top, axis=1)


def shares(amount, total, reach, slope, full):
    weights = [(1 << 20) // math.isqrt(standing ** slope) + 1 for standing in range(1, amount + 1)]
    largest = reach if full else min(reach, max(-(-total // amount), total * weights[0] // sum(weights)))
    least = 1 if total - largest >= amount - 1 else 0
    given, spare = [largest] + [least] * (amount - 1), total - largest - least * (amount - 1)
    while spare > 0:
        movable = [i for i in range(1, amount) if given[i] < largest] or [i for i in range(1, amount) if given[i] < reach]
        pool, remaining = sum([weights[i] for i in movable]), spare
        for i in movable:
            extra = min(reach - given[i], max(1, remaining * weights[i] // pool), spare)
            given[i] = given[i] + extra
            spare = spare - extra
    return np.array(given)


def normal_values(rng, extent, deviation, bound, cuts=(), kind=jnp.bfloat16):
    entries = jax.random.normal(rng, extent, jnp.float32) * deviation
    if len(cuts) > 0:
        entries = steps_of(rng, extent, cuts, -0.22, 0.18) * entries
    return jnp.clip(entries, min=-bound, max=bound).astype(kind)


def setup_inputs(seed: int = 0, part: int = 0) -> dict:
    key_of = jax.random.split(jax.random.key(seed), 12)
    own_keys = jax.random.split(jax.random.fold_in(key_of[11], part), 12)
    obs_owner_keys = jax.random.split(jax.random.fold_in(own_keys[0], 1), NOBS // OBS_DEV)
    obs_owner_turns = jax.random.permutation(jax.random.fold_in(own_keys[0], 3), NOBS // OBS_DEV)
    obs_owner = jax.vmap(lambda own, number: shared_out(jax.random.fold_in(own_keys[0], 2), own, number, OBS_DEV, N_LON, 1, CAP, 2))(obs_owner_keys, obs_owner_turns).reshape((NOBS, 1))
    obs_lonpos = touch_ends(jax.random.randint(own_keys[1], (NOBS,), 0, LON_DEV), jax.random.fold_in(own_keys[1], 1), 0, LON_DEV - 1).astype(jnp.int32)
    obs_lat = touch_ends(jax.random.randint(own_keys[2], (NOBS,), 0, NLAT), jax.random.fold_in(own_keys[2], 1), 0, NLAT - 1).astype(jnp.int32)
    obs_step = touch_ends(jax.random.randint(own_keys[3], (NOBS,), 1, NSTEP + 1), jax.random.fold_in(own_keys[3], 1), 1, NSTEP).astype(jnp.int32)
    obs_top = touch_ends(jax.random.randint(own_keys[4], (NOBS,), 1, L + 1), jax.random.fold_in(own_keys[4], 1), 1, L).astype(jnp.int32)
    innovation = normal_values(own_keys[5], (L, NOBS), 1.0, 6.0, ((1, 16),), jnp.float32)
    obs_weight = jnp.clip(jnp.exp(math.log(2.0) - 2.3025851 * jax.random.uniform(own_keys[6], (L, NOBS), jnp.float32) ** steps_of(own_keys[6], (L, NOBS), ((1, 16),), -0.2, 0.2)), 0.2, 2.0)
    wind_shift = touch_ends(jax.random.randint(key_of[7], (NSTEP, L, NLAT), -1, 2), jax.random.fold_in(key_of[7], 1), -1, 1).astype(jnp.int32)
    wind_frac = jnp.clip(jax.random.uniform(key_of[8], (NSTEP, L, NLAT), jnp.float32, 0.0, 1.0), 0.0, 1.0)
    vmix = draw_vmix(jax.random.fold_in(key_of[11], 71), part)
    hcoef = normal_values(key_of[10], (FIELDS, L), 0.5, 3.0, (), jnp.float32)
    return {"obs_owner": obs_owner, "obs_lonpos": obs_lonpos, "obs_lat": obs_lat, "obs_step": obs_step, "obs_top": obs_top, "innovation": innovation, "obs_weight": obs_weight, "wind_shift": wind_shift, "wind_frac": wind_frac, "vmix": vmix, "hcoef": hcoef}


HIGH = lax.Precision.HIGHEST


def stencil(shift_rows, frac_rows):
    weights = []
    for offset in range(-1, 3):
        weight = jnp.where(shift_rows == offset, 1.0 - frac_rows, 0.0) + jnp.where(shift_rows == offset - 1, frac_rows, 0.0)
        weights.append(weight[None, :, None, :])
    return weights


def advect(state_field, weights):
    summed = jnp.zeros_like(state_field)
    for position in range(4):
        summed = summed + weights[position] * jnp.roll(state_field, position - 1, axis=2)
    return summed


def advect_back(state_field, weights):
    summed = jnp.zeros_like(state_field)
    for position in range(4):
        summed = summed + weights[position] * jnp.roll(state_field, 1 - position, axis=2)
    return summed


def mix_levels(state_field, vmix):
    return jnp.einsum("flm,fmip->flip", vmix, state_field, precision=HIGH)


def mix_back(state_field, vmix):
    return jnp.einsum("fml,fmip->flip", vmix, state_field, precision=HIGH)


def reference(obs_owner, obs_lonpos, obs_lat, obs_step, obs_top, innovation, obs_weight, wind_shift, wind_frac, vmix, hcoef):
    longitude = (obs_owner[:, 0] * LON_DEV + obs_lonpos).astype(jnp.int32)
    level_iota = jnp.arange(L, dtype=jnp.int32)
    level_mask = level_iota[:, None] < obs_top[None, :]
    weights = [stencil(wind_shift[index], wind_frac[index]) for index in range(NSTEP)]

    def tangent(start):
        gathered = jnp.zeros((L, NOBS), jnp.float32)
        state_field = start
        for step_no in range(1, NSTEP + 1):
            state_field = mix_levels(advect(state_field, weights[step_no - 1]), vmix)
            column_sums = jnp.sum(hcoef[:, :, None, None] * state_field, axis=0)
            picked = column_sums[:, longitude, obs_lat]
            chosen = (obs_step == step_no)[None, :] & level_mask
            gathered = gathered + jnp.where(chosen, picked, 0.0)
        return gathered

    def forcing(departures, step_no):
        picked = jnp.where((obs_step == step_no)[None, :], departures, 0.0)
        spread = jnp.zeros((L, NLON, NLAT), jnp.float32).at[:, longitude, obs_lat].add(picked)
        return hcoef[:, :, None, None] * spread

    def adjoint(departures):
        adjoint_field = forcing(departures, NSTEP)
        for step_no in range(NSTEP, 0, -1):
            adjoint_field = advect_back(mix_back(adjoint_field, vmix), weights[step_no - 1])
            if step_no > 1:
                adjoint_field = adjoint_field + forcing(departures, step_no - 1)
        return adjoint_field

    right_side = adjoint(obs_weight * jnp.where(level_mask, innovation, 0.0))
    increment = jnp.zeros_like(right_side)
    residual = right_side
    direction = right_side
    norm_now = jnp.sum(residual * residual)
    for round_no in range(ITERS):
        image = direction + adjoint(obs_weight * tangent(direction))
        alpha = norm_now / jnp.sum(direction * image)
        increment = increment + alpha * direction
        residual = residual - alpha * image
        if round_no + 1 < ITERS:
            norm_next = jnp.sum(residual * residual)
            direction = residual + (norm_next / norm_now) * direction
            norm_now = norm_next
    return increment, residual
```

```python
import functools

import jax
import jax.numpy as jnp
from jax import lax
from jax.experimental import pallas as pl
from jax.experimental.pallas import tpu as pltpu
from jax.sharding import PartitionSpec as P

F32 = jnp.float32
BF16 = jnp.bfloat16
BAND = 8
LANE = 128
STEPS = 3
CHUNK = 32
VMEM_BYTES = 52 * 1024 * 1024

NN = (((1,), (0,)), ((), ()))
NT = (((1,), (1,)), ((), ()))


def dot(left, right, dims=NN):
    return lax.dot_general(left, right, dims, preferred_element_type=F32)


def halves(value):
    high = value.astype(BF16)
    return high, (value - high.astype(F32)).astype(BF16)


def thirds(value):
    high = value.astype(BF16)
    rest = value - high.astype(F32)
    middle = rest.astype(BF16)
    return high, middle, (rest - middle.astype(F32)).astype(BF16)


def fold(product):
    return product[:, :LANE] + product[:, LANE:]


def down(row, count):
    return jnp.broadcast_to(row, (LANE, row.shape[1])).T[:, :count]


def pack_kernel(owner, lonpos, lat, step, top, innovation, weight, out, w_rows, d_rows):
    devices, block, _ = out.shape
    count = owner.shape[1]
    slots = w_rows.shape[0]
    cap = slots // devices
    owners = owner[...].astype(F32)
    upright = down(owners, LANE)
    upright = jnp.concatenate([upright] * (count // LANE), axis=1)
    earlier = lax.broadcasted_iota(jnp.int32, (count, count), 0) < lax.broadcasted_iota(
        jnp.int32, (count, count), 1
    )
    same = jnp.where((upright == owners) & earlier, 1.0, 0.0)
    rank = jnp.sum(same, axis=0, keepdims=True)
    slot = (owners * cap + rank).astype(jnp.int32)
    onehot = jnp.where(
        lax.broadcasted_iota(jnp.int32, (slots, count), 0) == slot, 1.0, 0.0
    ).astype(BF16)
    seen = lax.broadcasted_iota(jnp.int32, (LANE, count), 0) < top[...]
    weights = jnp.where(seen, weight[...], 0.0)
    parts = thirds(weights) + thirds(weights * innovation[...])
    rows = dot(onehot, jnp.concatenate(parts, axis=0), NT)
    w_rows[...] = rows[:, 0:128] + rows[:, 128:256] + rows[:, 256:384]
    d_rows[...] = rows[:, 384:512] + rows[:, 512:640] + rows[:, 640:768]
    line = lax.broadcasted_iota(jnp.int32, (8, count), 0)
    facts = jnp.where(
        line == 0, lonpos[...], jnp.where(line == 1, lat[...], jnp.where(line == 2, step[...], 0))
    )
    facts = dot(facts.astype(F32).astype(BF16), onehot, NT)
    first = lax.broadcasted_iota(jnp.int32, (8, LANE), 0) == 0
    inside = lax.broadcasted_iota(jnp.int32, (8, LANE), 1) < cap
    for dest in range(devices):
        out[dest, 0:cap, :] = w_rows[dest * cap : (dest + 1) * cap, :]
        out[dest, cap : 2 * cap, :] = d_rows[dest * cap : (dest + 1) * cap, :]
        at = dest * cap // LANE * LANE
        tile = facts[:, at : at + LANE]
        if dest * cap != at:
            tile = pltpu.roll(tile, LANE - (dest * cap - at), 1)
        column = tile[0:1] * float(LANE) + tile[1:2]
        tile = jnp.where(first, column, tile[2:3])
        out[dest, 2 * cap : 2 * cap + 8, :] = jnp.where(inside, tile, 0.0)


def prepare_kernel(shift, frac, vmix, hcoef, mats, offs, fracs, scale):
    fields = vmix.shape[0]
    for t in range(STEPS):
        offs[t] = shift[t].astype(F32).T
        fracs[t] = frac[t].T
    bound = jnp.zeros((1, 1), F32)
    reach = jnp.zeros((1, LANE), F32)
    for f in range(fields):
        v = vmix[f]
        size = jnp.abs(v)
        over = jnp.max(jnp.sum(size, axis=0, keepdims=True), axis=1, keepdims=True)
        along = jnp.max(jnp.sum(size, axis=1, keepdims=True), axis=0, keepdims=True)
        bound = jnp.maximum(bound, over * along)
        row = hcoef[f : f + 1, :]
        reach = reach + row * row
        turned = v.T
        weighed = turned * row
        for kind, matrix in enumerate((v, weighed.T, turned, weighed)):
            high, low = halves(matrix)
            both = jnp.concatenate([high, low], axis=1)
            mats[kind, f] = jnp.concatenate([both, both], axis=0)
    rho = bound * bound * bound * jnp.max(reach, axis=1, keepdims=True) * 2.0
    rho = jnp.minimum(jnp.maximum(rho, 1e-18), 1e18)
    scale[...] = jnp.broadcast_to(1.0 / rho, (8, LANE))


def place_of(column, step):
    return (step - 1.0) * float(BAND * LANE) + column


def line_of(ref, first, count):
    return jnp.concatenate([ref[first + n : first + n + 1, :] for n in range(count)], axis=1)


def places(ref, slots):
    groups = slots // LANE
    return place_of(line_of(ref, slots, groups), line_of(ref, slots + groups, groups)).astype(
        jnp.int32
    )


def lat_onehot(place, first, count):
    rows = lax.broadcasted_iota(jnp.int32, (count, place.shape[1]), 0) + first
    return jnp.where((place & (LANE - 1)) == rows, 1.0, 0.0).astype(BF16)


def block_mask(place, block, count):
    wide = jnp.broadcast_to(place >> 7, (count, place.shape[1]))
    return jnp.where(wide == block, 1.0, 0.0).astype(BF16)


def edges_of(place, both):
    lats = lat_onehot(place, 0, LANE)
    first = lats * block_mask(place, (STEPS - 1) * BAND, LANE)
    last = lats * block_mask(place, STEPS * BAND - 1, LANE)
    return fold(dot(jnp.concatenate([first, last], axis=0), both))


def unpack_kernel(received, scale, w_out, ex_out, edge_out):
    devices = received.shape[0]
    slots = w_out.shape[0]
    cap = slots // devices
    per = LANE // cap
    groups = slots // LANE
    shrink = scale[0:1, :]
    lines = [jnp.zeros((8, LANE), F32) for _ in range(groups)]
    for source in range(devices):
        at = source * cap
        w_out[at : at + cap, :] = received[source, 0:cap, :] * shrink
        ex_out[at : at + cap, :] = received[source, cap : 2 * cap, :]
        tile = received[source, 2 * cap : 2 * cap + 8, :]
        if source % per:
            tile = pltpu.roll(tile, cap * (source % per), 1)
        lines[source // per] = lines[source // per] + tile
    for n in range(groups):
        ex_out[slots + n : slots + n + 1, :] = lines[n][0:1]
        ex_out[slots + groups + n : slots + groups + n + 1, :] = lines[n][1:2]
    place = places(ex_out, slots)
    both = jnp.concatenate(halves(ex_out[0:slots, :]), axis=1)
    edge_out[...] = edges_of(place, both)


def regions(begin, end):
    return [(begin - t, end + 2 * t) for t in range(1, STEPS + 1)]


def sweep_kernel(full, begin, end, *refs):
    if full:
        (left, own, right, m_left, m_own, m_right, e_left, e_right, mats, offs, fracs, hcoef, w,
         mom, out, z_out, edge_out, mom_out, *scratch) = refs
        sel, lats, masks, zs, z1, z2, lz, u, low, ys, reads = scratch
    else:
        (left, own, right, m_left, m_own, m_right, mats, offs, fracs, hcoef, out, *scratch) = refs
        sel, lats, masks, zs, z1, z2, lz, u, low = scratch
    fields = mats.shape[1]
    slots = zs.shape[1]
    spans = regions(begin, end)
    rows_of = (left, own, right)
    place = [places(ref, slots) for ref in (m_left, m_own, m_right)]
    blocks = []
    for band in range(3):
        shift = (band - 1) * BAND
        blocks.append(
            [
                (t, i, i + shift - spans[t - 1][0])
                for t in range(1, STEPS + 1)
                for i in range(BAND)
                if spans[t - 1][0] <= i + shift < spans[t - 1][1]
            ]
        )
        high, lo = halves(rows_of[band][0:slots, :])
        zs[band, :, 0:LANE] = high
        zs[band, :, LANE:] = lo
        lats[band] = lat_onehot(place[band], 0, LANE)
        for t, i, _ in blocks[band]:
            masks[band, (t - 1) * BAND + i] = block_mask(place[band], (t - 1) * BAND + i, 16)

    wide3 = spans[2][1] - spans[2][0]

    def split_to(ref, at, value):
        high, lo = halves(value)
        ref[at : at + CHUNK, 0:LANE] = high
        ref[at : at + CHUNK, LANE:] = lo

    def chunk(c, sums):
        p0 = pl.multiple_of(c * CHUNK, CHUNK)
        here = pl.ds(p0, CHUNK)
        for band in range(3):
            count = len(blocks[band])
            for n, (t, i, _) in enumerate(blocks[band]):
                mask = masks[band, (t - 1) * BAND + i]
                mask = jnp.concatenate([mask] * (CHUNK // 16), axis=0)
                sel[band, n * CHUNK : (n + 1) * CHUNK, :] = lats[band, here, :] * mask
            dense = fold(dot(sel[band, 0 : count * CHUNK, :], zs[band]))
            for n, (t, i, at) in enumerate(blocks[band]):
                slab = dense[n * CHUNK : (n + 1) * CHUNK]
                if t == 3:
                    split_to(lz, at * CHUNK, slab)
                else:
                    (z1 if t == 1 else z2)[at] = slab
        if full:
            split_to(lz, 0, e_left[here, :])
            split_to(lz, (wide3 - 1) * CHUNK, e_right[here, :])

        def multiply(source, f, kind, wide):
            product = fold(dot(source[0 : wide * CHUNK, :], mats[kind, f]))
            u[f, 0:wide] = product.reshape(wide, CHUNK, LANE)

        def advect(f, t, wide, forward, consume):
            a = fracs[t - 1, here, :]
            s = offs[t - 1, here, :]
            if forward:
                s = -s
            back_one = s < 0.0
            same = s == 0.0
            u1, u2 = u[f, 1], u[f, 2]
            h = jnp.where(back_one, u[f, 0], jnp.where(same, u1, u2))
            for j in range(wide - 3):
                u3 = u[f, j + 3]
                h2 = jnp.where(back_one, u1, jnp.where(same, u2, u3))
                if forward:
                    consume(j, h2 + a * (h - h2))
                else:
                    consume(j, h + a * (h2 - h))
                u1, u2, h = u2, u3, h2

        wide = wide3
        for t in (3, 2, 1):
            for f in range(fields):
                if t == 3:
                    multiply(lz, f, 1, wide)
                else:
                    multiply(low.at[f], f, 0, wide)
                if t > 1:
                    force = z2 if t == 3 else z1
                    row = hcoef[f : f + 1, :]

                    def keep(j, value, f=f, force=force, row=row):
                        split_to(low.at[f], j * CHUNK, value + row * force[j])

                else:

                    def keep(j, value, f=f):
                        lon = j + begin
                        if full:
                            u[f, j] = value
                        if 0 <= lon < BAND:
                            out[f, lon, here, :] = value

                advect(f, t, wide, False, keep)
            wide = wide - 3
        if not full:
            return sums

        seen = begin
        y_now = None
        for t in (1, 2, 3):
            seen = seen + 2
            y_now = [None] * BAND
            total = None
            for f in range(fields):

                def keep(j, value, f=f):
                    split_to(low.at[f], j * CHUNK, value)

                if t == 1:
                    for lon in range(BAND):
                        cell = u[f, lon - begin]
                        sums = sums + jnp.sum(
                            (cell * cell).reshape(CHUNK // 8, 8, LANE), axis=0
                        )
                advect(f, t, wide, True, keep)
                if t < 3:
                    multiply(low.at[f], f, 2, wide - 3)
                    row = hcoef[f : f + 1, :]
                    for lon in range(BAND):
                        term = row * u[f, lon - seen]
                        y_now[lon] = term if f == 0 else y_now[lon] + term
                else:
                    term = dot(low[f, 0 : BAND * CHUNK, :], mats[3, f])
                    total = term if f == 0 else total + term
            if t == 3:
                total = fold(total)
                y_now = [total[lon * CHUNK : (lon + 1) * CHUNK] for lon in range(BAND)]
            for lon in range(BAND):
                high, lo = halves(y_now[lon])
                to = pl.ds(((t - 1) * BAND + lon) * LANE + p0, CHUNK)
                ys[to, 0:LANE] = high
                ys[to, LANE:] = lo
            wide = wide - 3
        return sums

    sums = lax.fori_loop(0, LANE // CHUNK, chunk, jnp.zeros((8, LANE), F32))
    if not full:
        return

    upright = jnp.concatenate(
        [down(place[1][:, n : n + LANE].astype(F32), LANE) for n in range(0, slots, LANE)], axis=0
    )
    away = upright - lax.broadcasted_iota(jnp.int32, (slots, LANE), 1).astype(F32)
    for block in range(STEPS * BAND):
        reads[:, block * LANE : (block + 1) * LANE] = jnp.where(
            away == float(block * LANE), 1.0, 0.0
        ).astype(BF16)
    y = fold(dot(reads[...], ys[...]))
    z = w[...] * y
    z_out[...] = z
    curve = jnp.sum((z * y).reshape(slots // 8, 8, LANE), axis=0)
    edge_out[...] = edges_of(place[1], jnp.concatenate(halves(z), axis=1))
    line = lax.broadcasted_iota(jnp.int32, (8, LANE), 0)
    one = jnp.sum(sums, axis=0, keepdims=True)
    two = jnp.sum(curve, axis=0, keepdims=True)
    mom_out[...] = jnp.where(line == 0, one, jnp.where(line == 1, two, 0.0))
    mom_out[2:4, :] = mom[0:2, :]


def combine_kernel(moments, scale, b, c0, c1, increment, residual):
    total = jnp.sum(moments[...], axis=0)
    total = jnp.sum(total, axis=1, keepdims=True)
    base = total[2:3]
    m1 = total[3:4] / base
    m2 = total[0:1] / base
    m3 = total[1:2] / base
    eps = scale[0:1, 0:1]
    ap = 1.0 / (eps + m1)
    alpha = eps * ap
    beta = (m2 - m1 * m1) * ap * ap
    u = 1.0 + beta - alpha
    curve = eps * (u * u - 2.0 * u * ap * m1 + ap * ap * m2) + (
        u * u * m1 - 2.0 * u * ap * m2 + ap * ap * m3
    )
    a2p = beta / curve
    a2 = eps * a2p
    inc_b = alpha + a2 * u
    inc_c = -(a2 * ap)
    res_b = 1.0 - alpha - a2 * u
    res_c = a2 * ap - ap - a2p * u
    res_d = a2p * ap
    for lon in range(BAND):
        b_now, c_now = b[0, lon], c0[0, lon]
        to = pl.ds(lon, LANE, stride=BAND)
        increment[0, to, :] = (inc_b * b_now + inc_c * c_now).T
        residual[0, to, :] = (res_b * b_now + res_c * c_now + res_d * c1[0, lon]).T


def params(**more):
    return pltpu.CompilerParams(vmem_limit_bytes=VMEM_BYTES, **more)


def shards(
    obs_owner, obs_lonpos, obs_lat, obs_step, obs_top, innovation, obs_weight,
    wind_shift, wind_frac, vmix, hcoef,
):
    devices = lax.axis_size("lon")
    fields = vmix.shape[0]
    count = obs_owner.shape[0]
    cap = max(2, 2 * count // devices)
    slots = devices * cap
    shape = jax.ShapeDtypeStruct
    state = shape((fields, BAND, LANE, LANE), F32)
    rows = shape((slots, LANE), F32)
    edge = shape((2 * LANE, LANE), F32)
    small = shape((8, LANE), F32)

    send = pl.pallas_call(
        pack_kernel,
        out_shape=shape((devices, 2 * cap + 8, LANE), F32),
        scratch_shapes=[pltpu.VMEM((slots, LANE), F32)] * 2,
        compiler_params=params(),
        name="pack",
    )(
        obs_owner.reshape(1, count), obs_lonpos.reshape(1, count), obs_lat.reshape(1, count),
        obs_step.reshape(1, count), obs_top.reshape(1, count), innovation, obs_weight,
    )
    mats, offs, fracs, scale = pl.pallas_call(
        prepare_kernel,
        out_shape=(
            shape((4, fields, 2 * LANE, 2 * LANE), BF16),
            shape((STEPS, LANE, LANE), F32),
            shape((STEPS, LANE, LANE), F32),
            small,
        ),
        compiler_params=params(),
        name="prepare",
    )(wind_shift, wind_frac, vmix, hcoef)
    received = lax.all_to_all(send, "lon", split_axis=0, concat_axis=0, tiled=True)
    w, rows_d, edge_d = pl.pallas_call(
        unpack_kernel,
        out_shape=(rows, shape((slots + 8, LANE), F32), edge),
        compiler_params=params(),
        name="unpack",
    )(received, scale)

    def along(value, hop):
        return lax.ppermute(value, "lon", [(i, (i + hop) % devices) for i in range(devices)])

    def swap(value, edges):
        near = (along(value, 1), value, along(value, -1))
        if edges is None:
            return near, ()
        return near, (along(edges[LANE:], 2), along(edges[:LANE], -2))

    def scratch(full, begin, end):
        wide = [b - a for a, b in regions(begin, end)]
        shapes = [
            pltpu.VMEM((3, STEPS * BAND * CHUNK, slots), BF16),
            pltpu.VMEM((3, LANE, slots), BF16),
            pltpu.VMEM((3, STEPS * BAND, 16, slots), BF16),
            pltpu.VMEM((3, slots, 2 * LANE), BF16),
            pltpu.VMEM((wide[0], CHUNK, LANE), F32),
            pltpu.VMEM((wide[1], CHUNK, LANE), F32),
            pltpu.VMEM((wide[2] * CHUNK, 2 * LANE), BF16),
            pltpu.VMEM((fields, wide[2], CHUNK, LANE), F32),
            pltpu.VMEM((fields, wide[1] * CHUNK, 2 * LANE), BF16),
        ]
        if full:
            shapes.append(pltpu.VMEM((STEPS * BAND * LANE, 2 * LANE), BF16))
            shapes.append(pltpu.VMEM((slots, STEPS * BAND * LANE), BF16))
        return shapes

    def sweep(near, far, facts, mom):
        return pl.pallas_call(
            functools.partial(sweep_kernel, True, -6, BAND + 3),
            out_shape=(state, rows, edge, small),
            scratch_shapes=scratch(True, -6, BAND + 3),
            compiler_params=params(),
            name="sweep",
        )(*near, *facts, *far, mats, offs, fracs, hcoef, w, mom)

    facts, far = swap(rows_d, edge_d)
    b, z0, edge0, mom = sweep(facts, far, facts, jnp.zeros((8, LANE), F32))
    near, far = swap(z0, edge0)
    c0, z1, _, mom = sweep(near, far, facts, mom)
    moments = lax.all_gather(mom, "lon")
    near, _ = swap(z1, None)
    c1 = pl.pallas_call(
        functools.partial(sweep_kernel, False, 0, BAND),
        out_shape=state,
        scratch_shapes=scratch(False, 0, BAND),
        compiler_params=params(),
        name="last_sweep",
    )(*near, *facts, mats, offs, fracs, hcoef)

    block = pl.BlockSpec((1, BAND, LANE, LANE), lambda f: (f, 0, 0, 0))
    done = pl.BlockSpec((1, BAND * LANE, LANE), lambda f: (f, 0, 0))
    flat = shape((fields, LANE * BAND, LANE), F32)
    increment, residual = pl.pallas_call(
        combine_kernel,
        out_shape=(flat, flat),
        grid=(fields,),
        in_specs=[
            pl.BlockSpec((devices, 8, LANE), lambda f: (0, 0, 0)),
            pl.BlockSpec((8, LANE), lambda f: (0, 0)),
            block, block, block,
        ],
        out_specs=(done, done),
        compiler_params=params(),
        name="combine",
    )(moments, scale, b, c0, c1)
    whole = (fields, LANE, BAND, LANE)
    return increment.reshape(whole), residual.reshape(whole)


def solution(mesh):
    profile = P(("member", "lon"))
    field = P("member", None, "lon", None)
    return jax.shard_map(
        shards,
        mesh=mesh,
        in_specs=(P("lon", "member"),) + (profile,) * 4 + (P("member", "lon"),) * 2 + (P(),) * 4,
        out_specs=(field, field),
        check_vma=False,
    )
```

```python
import functools

import jax
import jax.numpy as jnp
from jax import lax
from jax.experimental import pallas as pl
from jax.experimental.pallas import tpu as pltpu
from jax.sharding import PartitionSpec as P

F32 = jnp.float32
BF16 = jnp.bfloat16
BAND = 8
LANE = 128
STEPS = 3
PART = 16
VMEM_BYTES = 52 * 1024 * 1024

NN = (((1,), (0,)), ((), ()))
NT = (((1,), (1,)), ((), ()))


def dot(left, right, dims=NN):
    return lax.dot_general(left, right, dims, preferred_element_type=F32)


def halves(value):
    high = value.astype(BF16)
    return high, (value - high.astype(F32)).astype(BF16)


def thirds(value):
    high = value.astype(BF16)
    rest = value - high.astype(F32)
    middle = rest.astype(BF16)
    return high, middle, (rest - middle.astype(F32)).astype(BF16)


def fold(product):
    return product[:, :LANE] + product[:, LANE:]


def down(row, count):
    return jnp.broadcast_to(row, (LANE, row.shape[1])).T[:, :count]


def pack_kernel(*refs):
    sources, (out, w_rows, d_rows), held = refs[:7], refs[7:10], refs[10:17]
    copies = [
        pltpu.make_async_copy(source, place, refs[17].at[n])
        for n, (source, place) in enumerate(zip(sources, held))
    ]
    for copy in copies:
        copy.start()
    for copy in copies:
        copy.wait()
    owner, lonpos, lat, step, top, innovation, weight = held
    devices, block, _ = out.shape
    count = owner.shape[1]
    slots = w_rows.shape[0]
    cap = slots // devices
    owners = owner[...].astype(F32)
    upright = down(owners, LANE)
    upright = jnp.concatenate([upright] * (count // LANE), axis=1)
    earlier = lax.broadcasted_iota(jnp.int32, (count, count), 0) < lax.broadcasted_iota(
        jnp.int32, (count, count), 1
    )
    same = jnp.where((upright == owners) & earlier, 1.0, 0.0)
    rank = jnp.sum(same, axis=0, keepdims=True)
    slot = (owners * cap + rank).astype(jnp.int32)
    onehot = jnp.where(
        lax.broadcasted_iota(jnp.int32, (slots, count), 0) == slot, 1.0, 0.0
    ).astype(BF16)
    seen = lax.broadcasted_iota(jnp.int32, (LANE, count), 0) < top[...]
    weights = jnp.where(seen, weight[...], 0.0)
    parts = thirds(weights) + thirds(weights * innovation[...])
    rows = dot(onehot, jnp.concatenate(parts, axis=0), NT)
    w_rows[...] = rows[:, 0:128] + rows[:, 128:256] + rows[:, 256:384]
    d_rows[...] = rows[:, 384:512] + rows[:, 512:640] + rows[:, 640:768]
    line = lax.broadcasted_iota(jnp.int32, (8, count), 0)
    facts = jnp.where(
        line == 0, lonpos[...], jnp.where(line == 1, lat[...], jnp.where(line == 2, step[...], 0))
    )
    facts = dot(facts.astype(F32).astype(BF16), onehot, NT)
    first = lax.broadcasted_iota(jnp.int32, (8, LANE), 0) == 0
    inside = lax.broadcasted_iota(jnp.int32, (8, LANE), 1) < cap
    for dest in range(devices):
        out[dest, 0:cap, :] = w_rows[dest * cap : (dest + 1) * cap, :]
        out[dest, cap : 2 * cap, :] = d_rows[dest * cap : (dest + 1) * cap, :]
        at = dest * cap // LANE * LANE
        tile = facts[:, at : at + LANE]
        if dest * cap != at:
            tile = pltpu.roll(tile, LANE - (dest * cap - at), 1)
        column = tile[0:1] * float(LANE) + tile[1:2]
        tile = jnp.where(first, column, tile[2:3])
        out[dest, 2 * cap : 2 * cap + 8, :] = jnp.where(inside, tile, 0.0)


def prepare_kernel(shift, frac, vmix, hcoef, mats, offs, fracs, scale):
    fields = vmix.shape[0]
    for t in range(STEPS):
        offs[t] = shift[t].astype(F32).T
        fracs[t] = frac[t].T
    bound = jnp.zeros((1, 1), F32)
    reach = jnp.zeros((1, LANE), F32)
    for f in range(fields):
        v = vmix[f]
        size = jnp.abs(v)
        over = jnp.max(jnp.sum(size, axis=0, keepdims=True), axis=1, keepdims=True)
        along = jnp.max(jnp.sum(size, axis=1, keepdims=True), axis=0, keepdims=True)
        bound = jnp.maximum(bound, over * along)
        row = hcoef[f : f + 1, :]
        reach = reach + row * row
        turned = v.T
        weighed = turned * row
        for kind, matrix in enumerate((v, weighed.T, turned, weighed)):
            high, low = halves(matrix)
            both = jnp.concatenate([high, low], axis=1)
            mats[kind, f] = jnp.concatenate([both, both], axis=0)
    rho = bound * bound * bound * jnp.max(reach, axis=1, keepdims=True) * 2.0
    rho = jnp.minimum(jnp.maximum(rho, 1e-18), 1e18)
    scale[...] = jnp.broadcast_to(1.0 / rho, (8, LANE))


def place_of(column, step):
    return (step - 1.0) * float(BAND * LANE) + column


def line_of(ref, first, count):
    return jnp.concatenate([ref[first + n : first + n + 1, :] for n in range(count)], axis=1)


def places(ref, slots):
    groups = slots // LANE
    return place_of(line_of(ref, slots, groups), line_of(ref, slots + groups, groups)).astype(
        jnp.int32
    )


def lat_onehot(place, first, count):
    rows = lax.broadcasted_iota(jnp.int32, (count, place.shape[1]), 0) + first
    return jnp.where((place & (LANE - 1)) == rows, 1.0, 0.0).astype(BF16)


def block_mask(place, block, count):
    wide = jnp.broadcast_to(place >> 7, (count, place.shape[1]))
    return jnp.where(wide == block, 1.0, 0.0).astype(BF16)


def edges_of(place, both):
    lats = lat_onehot(place, 0, LANE)
    first = lats * block_mask(place, (STEPS - 1) * BAND, LANE)
    last = lats * block_mask(place, STEPS * BAND - 1, LANE)
    return fold(dot(jnp.concatenate([first, last], axis=0), both))


def unpack_kernel(received, scale, w_out, ex_out, edge_out):
    devices = received.shape[0]
    slots = w_out.shape[0]
    cap = slots // devices
    per = LANE // cap
    groups = slots // LANE
    shrink = scale[0:1, :]
    lines = [jnp.zeros((8, LANE), F32) for _ in range(groups)]
    for source in range(devices):
        at = source * cap
        w_out[at : at + cap, :] = received[source, 0:cap, :] * shrink
        ex_out[at : at + cap, :] = received[source, cap : 2 * cap, :]
        tile = received[source, 2 * cap : 2 * cap + 8, :]
        if source % per:
            tile = pltpu.roll(tile, cap * (source % per), 1)
        lines[source // per] = lines[source // per] + tile
    for n in range(groups):
        ex_out[slots + n : slots + n + 1, :] = lines[n][0:1]
        ex_out[slots + groups + n : slots + groups + n + 1, :] = lines[n][1:2]
    place = places(ex_out, slots)
    both = jnp.concatenate(halves(ex_out[0:slots, :]), axis=1)
    edge_out[...] = edges_of(place, both)


def regions(begin, end):
    return [(begin - t, end + 2 * t) for t in range(1, STEPS + 1)]


def sweep_kernel(full, chunk_size, begin, end, *refs):
    CHUNK = chunk_size
    if full:
        (odd, inner, own, outer, m_inner, m_own, m_outer, e_left, e_right, mats, offs, fracs,
         hcoef, w, out, z_out, edge_out, *scratch) = refs
        sel, lats, masks, zs, z1, z2, lz, u, low, ys, reads = scratch
    else:
        (odd, inner, own, outer, m_inner, m_own, m_outer, mats, offs, fracs, hcoef, out,
         *scratch) = refs
        sel, lats, masks, zs, z1, z2, lz, u, low = scratch
    fields = mats.shape[1]
    slots = zs.shape[1]
    spans = regions(begin, end)
    swapped = odd[0]

    def choose(one, other):
        return jnp.where(jnp.broadcast_to(swapped, one.shape) == 1, one, other)

    near = (inner[0:slots, :], outer[0:slots, :])
    rows_of = (choose(near[0], near[1]), own[0:slots, :], choose(near[1], near[0]))
    near = (places(m_inner, slots), places(m_outer, slots))
    place = (choose(near[0], near[1]), places(m_own, slots), choose(near[1], near[0]))
    blocks = []
    for band in range(3):
        shift = (band - 1) * BAND
        blocks.append(
            [
                (t, i, i + shift - spans[t - 1][0])
                for t in range(1, STEPS + 1)
                for i in range(BAND)
                if spans[t - 1][0] <= i + shift < spans[t - 1][1]
            ]
        )
        high, lo = halves(rows_of[band])
        zs[band, :, 0:LANE] = high
        zs[band, :, LANE:] = lo
        lats[band] = lat_onehot(place[band], 0, LANE)
        for t, i, _ in blocks[band]:
            masks[band, (t - 1) * BAND + i] = block_mask(place[band], (t - 1) * BAND + i, 16)

    wide3 = spans[2][1] - spans[2][0]

    def split_to(ref, at, value):
        high, lo = halves(value)
        ref[at : at + value.shape[0], 0:LANE] = high
        ref[at : at + value.shape[0], LANE:] = lo

    def chunk(c, sums):
        p0 = pl.multiple_of(c * CHUNK, CHUNK)
        here = pl.ds(p0, CHUNK)
        for band in range(3):
            count = len(blocks[band])
            for n, (t, i, _) in enumerate(blocks[band]):
                mask = masks[band, (t - 1) * BAND + i]
                mask = jnp.concatenate([mask] * (CHUNK // 16), axis=0)
                sel[band, n * CHUNK : (n + 1) * CHUNK, :] = lats[band, here, :] * mask
            dense = fold(dot(sel[band, 0 : count * CHUNK, :], zs[band]))
            for n, (t, i, at) in enumerate(blocks[band]):
                slab = dense[n * CHUNK : (n + 1) * CHUNK]
                if t == 3:
                    split_to(lz, at * CHUNK, slab)
                else:
                    (z1 if t == 1 else z2)[at] = slab
        if full:
            split_to(lz, 0, e_left[here, :])
            split_to(lz, (wide3 - 1) * CHUNK, e_right[here, :])

        def multiply(source, f, kind, wide):
            product = fold(dot(source[0 : wide * CHUNK, :], mats[kind, f]))
            u[f, 0:wide] = product.reshape(wide, CHUNK, LANE)

        def advect(f, t, wide, forward, consume):
            for r in range(0, CHUNK, PART):
                part = slice(r, r + PART)
                a = fracs[t - 1, pl.ds(p0 + r, PART), :]
                s = offs[t - 1, pl.ds(p0 + r, PART), :]
                if forward:
                    s = -s
                back_one = s < 0.0
                same = s == 0.0
                u1, u2 = u[f, 1, part], u[f, 2, part]
                h = jnp.where(back_one, u[f, 0, part], jnp.where(same, u1, u2))
                for j in range(wide - 3):
                    u3 = u[f, j + 3, part]
                    h2 = jnp.where(back_one, u1, jnp.where(same, u2, u3))
                    if forward:
                        consume(j, r, h2 + a * (h - h2))
                    else:
                        consume(j, r, h + a * (h2 - h))
                    u1, u2, h = u2, u3, h2

        wide = wide3
        for t in (3, 2, 1):
            for f in range(fields):
                if t == 3:
                    multiply(lz, f, 1, wide)
                else:
                    multiply(low.at[f], f, 0, wide)
                if t > 1:
                    force = z2 if t == 3 else z1
                    row = hcoef[f : f + 1, :]

                    def keep(j, r, value, f=f, force=force, row=row):
                        value = value + row * force[j, r : r + PART]
                        split_to(low.at[f], j * CHUNK + r, value)

                else:

                    def keep(j, r, value, f=f):
                        lon = j + begin
                        if full:
                            u[f, j, r : r + PART] = value
                        if 0 <= lon < BAND:
                            out[f, lon, pl.ds(p0 + r, PART), :] = value

                advect(f, t, wide, False, keep)
            wide = wide - 3
        if not full:
            return sums

        seen = begin
        y_now = None
        for t in (1, 2, 3):
            seen = seen + 2
            y_now = [None] * BAND
            total = None
            for f in range(fields):

                def keep(j, r, value, f=f):
                    split_to(low.at[f], j * CHUNK + r, value)

                if t == 1:
                    for lon in range(BAND):
                        cell = u[f, lon - begin]
                        sums = sums + jnp.sum(
                            (cell * cell).reshape(CHUNK // 8, 8, LANE), axis=0
                        )
                advect(f, t, wide, True, keep)
                if t < 3:
                    multiply(low.at[f], f, 2, wide - 3)
                    row = hcoef[f : f + 1, :]
                    for lon in range(BAND):
                        term = row * u[f, lon - seen]
                        y_now[lon] = term if f == 0 else y_now[lon] + term
                else:
                    term = dot(low[f, 0 : BAND * CHUNK, :], mats[3, f])
                    total = term if f == 0 else total + term
            if t == 3:
                total = fold(total)
                y_now = [total[lon * CHUNK : (lon + 1) * CHUNK] for lon in range(BAND)]
            for lon in range(BAND):
                high, lo = halves(y_now[lon])
                to = pl.ds(((t - 1) * BAND + lon) * LANE + p0, CHUNK)
                ys[to, 0:LANE] = high
                ys[to, LANE:] = lo
            wide = wide - 3
        return sums

    sums = lax.fori_loop(0, LANE // CHUNK, chunk, jnp.zeros((8, LANE), F32))
    if not full:
        return

    upright = jnp.concatenate(
        [down(place[1][:, n : n + LANE].astype(F32), LANE) for n in range(0, slots, LANE)], axis=0
    )
    away = upright - lax.broadcasted_iota(jnp.int32, (slots, LANE), 1).astype(F32)
    for block in range(STEPS * BAND):
        reads[:, block * LANE : (block + 1) * LANE] = jnp.where(
            away == float(block * LANE), 1.0, 0.0
        ).astype(BF16)
    y = fold(dot(reads[...], ys[...]))
    z = w[...] * y
    z_out[0:slots, :] = z
    curve = jnp.sum((z * y).reshape(slots // 8, 8, LANE), axis=0)
    edge_out[...] = edges_of(place[1], jnp.concatenate(halves(z), axis=1))
    line = lax.broadcasted_iota(jnp.int32, (8, LANE), 0)
    one = jnp.sum(sums, axis=0, keepdims=True)
    two = jnp.sum(curve, axis=0, keepdims=True)
    z_out[slots : slots + 8, :] = jnp.where(line == 0, one, jnp.where(line == 1, two, 0.0))
    z_out[slots + 2 : slots + 4, :] = own[slots : slots + 2, :]


def turn_kernel(source, out):
    for lon in range(BAND):
        out[0, lon] = source[0, lon].T


def combine_kernel(*refs):
    *moments, scale, b, c0, c1, increment, residual = refs
    total = moments[0][...]
    for part in moments[1:]:
        total = total + part[...]
    total = jnp.sum(total, axis=1, keepdims=True)
    base = total[2:3]
    m1 = total[3:4] / base
    m2 = total[0:1] / base
    m3 = total[1:2] / base
    eps = scale[0:1, 0:1]
    ap = 1.0 / (eps + m1)
    alpha = eps * ap
    beta = (m2 - m1 * m1) * ap * ap
    u = 1.0 + beta - alpha
    curve = eps * (u * u - 2.0 * u * ap * m1 + ap * ap * m2) + (
        u * u * m1 - 2.0 * u * ap * m2 + ap * ap * m3
    )
    a2p = beta / curve
    a2 = eps * a2p
    inc_b = alpha + a2 * u
    inc_c = -(a2 * ap)
    res_b = 1.0 - alpha - a2 * u
    res_c = a2 * ap - ap - a2p * u
    res_d = a2p * ap
    for lon in range(BAND):
        b_now, c_now = b[0, lon], c0[0, lon]
        to = pl.ds(lon, LANE, stride=BAND)
        increment[0, to, :] = inc_b * b_now + inc_c * c_now
        residual[0, to, :] = res_b * b_now + res_c * c_now + res_d * c1[0, lon].T


def params(**more):
    return pltpu.CompilerParams(vmem_limit_bytes=VMEM_BYTES, **more)


def shards(
    obs_owner, obs_lonpos, obs_lat, obs_step, obs_top, innovation, obs_weight,
    wind_shift, wind_frac, vmix, hcoef,
):
    devices = lax.axis_size("lon")
    fields = vmix.shape[0]
    count = obs_owner.shape[0]
    cap = max(2, 2 * count // devices)
    slots = devices * cap
    shape = jax.ShapeDtypeStruct
    state = shape((fields, BAND, LANE, LANE), F32)
    rows = shape((slots, LANE), F32)
    edge = shape((2 * LANE, LANE), F32)
    small = shape((8, LANE), F32)
    more_rows = shape((slots + 8, LANE), F32)

    send = pl.pallas_call(
        pack_kernel,
        out_shape=shape((devices, 2 * cap + 8, LANE), F32),
        in_specs=[pl.BlockSpec(memory_space=pltpu.HBM)] * 7,
        scratch_shapes=[pltpu.VMEM((slots, LANE), F32)] * 2
        + [pltpu.VMEM((1, count), jnp.int32)] * 5
        + [pltpu.VMEM((LANE, count), F32)] * 2
        + [pltpu.SemaphoreType.DMA((7,))],
        compiler_params=params(),
        name="pack",
    )(
        obs_owner.reshape(1, count), obs_lonpos.reshape(1, count), obs_lat.reshape(1, count),
        obs_step.reshape(1, count), obs_top.reshape(1, count), innovation, obs_weight,
    )
    mats, offs, fracs, scale = pl.pallas_call(
        prepare_kernel,
        out_shape=(
            shape((4, fields, 2 * LANE, 2 * LANE), BF16),
            shape((STEPS, LANE, LANE), F32),
            shape((STEPS, LANE, LANE), F32),
            small,
        ),
        compiler_params=params(),
        name="prepare",
    )(wind_shift, wind_frac, vmix, hcoef)
    received = lax.all_to_all(send, "lon", split_axis=0, concat_axis=0, tiled=True)
    w, rows_d, edge_d = pl.pallas_call(
        unpack_kernel,
        out_shape=(rows, shape((slots + 8, LANE), F32), edge),
        compiler_params=params(),
        name="unpack",
    )(received, scale)

    def along(value, hop):
        return lax.ppermute(value, "lon", [(i, (i + hop) % devices) for i in range(devices)])

    def swap(value, first):
        pairs = [((i + first) % devices, (i + 1 + first) % devices) for i in range(0, devices, 2)]
        return lax.ppermute(value, "lon", pairs + [(b, a) for a, b in pairs])

    def near(value):
        return swap(value, 0), value, swap(value, 1)

    def far(edges):
        return along(edges[LANE:], 2), along(edges[:LANE], -2)

    def scratch(full, size, begin, end):
        wide = [b - a for a, b in regions(begin, end)]
        shapes = [
            pltpu.VMEM((3, STEPS * BAND * size, slots), BF16),
            pltpu.VMEM((3, LANE, slots), BF16),
            pltpu.VMEM((3, STEPS * BAND, 16, slots), BF16),
            pltpu.VMEM((3, slots, 2 * LANE), BF16),
            pltpu.VMEM((wide[0], size, LANE), F32),
            pltpu.VMEM((wide[1], size, LANE), F32),
            pltpu.VMEM((wide[2] * size, 2 * LANE), BF16),
            pltpu.VMEM((fields, wide[2], size, LANE), F32),
            pltpu.VMEM((fields, wide[1] * size, 2 * LANE), BF16),
        ]
        if full:
            shapes.append(pltpu.VMEM((STEPS * BAND * LANE, 2 * LANE), BF16))
            shapes.append(pltpu.VMEM((slots, STEPS * BAND * LANE), BF16))
        return shapes

    def specs(count):
        return [pl.BlockSpec(memory_space=pltpu.SMEM)] + [
            pl.BlockSpec(memory_space=pltpu.VMEM)
        ] * count

    def cost(columns):
        return pl.CostEstimate(
            flops=columns * fields * LANE * 8 * LANE * LANE,
            bytes_accessed=8 * 1024 * 1024,
            transcendentals=0,
        )

    odd = (lax.axis_index("lon") % 2).reshape(1)

    def sweep(rows_near, edges, facts, size):
        return pl.pallas_call(
            functools.partial(sweep_kernel, True, size, -6, BAND + 3),
            out_shape=(state, more_rows, edge),
            in_specs=specs(13),
            scratch_shapes=scratch(True, size, -6, BAND + 3),
            compiler_params=params(),
            cost_estimate=cost(130),
            name="sweep",
        )(odd, *rows_near, *facts, *far(edges), mats, offs, fracs, hcoef, w)

    block = pl.BlockSpec((1, BAND, LANE, LANE), lambda f: (f, 0, 0, 0))

    def turn(value):
        return pl.pallas_call(
            turn_kernel,
            out_shape=state,
            grid=(fields,),
            in_specs=[block],
            out_specs=block,
            compiler_params=params(),
            cost_estimate=cost(8),
            name="turn",
        )(value)

    facts = near(rows_d)
    b, z0, edge0 = sweep(facts, edge_d, facts, 64)
    c0, z1, _ = sweep(near(z0), edge0, facts, 32)
    last = near(z1)
    c1 = pl.pallas_call(
        functools.partial(sweep_kernel, False, 64, 0, BAND),
        out_shape=state,
        in_specs=specs(10),
        scratch_shapes=scratch(False, 64, 0, BAND),
        compiler_params=params(),
        cost_estimate=cost(60),
        name="last_sweep",
    )(odd, *last, *facts, mats, offs, fracs, hcoef)

    single = z1[slots:]
    window = last[0][slots:] + single + last[2][slots:]
    covered, parts = 3, [window]
    while devices // covered > 1:
        window = functools.reduce(jnp.add, parts)
        count_of = min(devices // covered, 7)
        parts = [window] + [along(window, -k * covered) for k in range(1, count_of)]
        covered = covered * count_of
    parts = parts + [along(single, -(k - 1)) for k in range(covered, devices)]

    done = pl.BlockSpec((1, BAND * LANE, LANE), lambda f: (f, 0, 0))
    flat = shape((fields, LANE * BAND, LANE), F32)
    increment, residual = pl.pallas_call(
        combine_kernel,
        out_shape=(flat, flat),
        grid=(fields,),
        in_specs=[pl.BlockSpec((8, LANE), lambda f: (0, 0))] * (len(parts) + 1) + [block] * 3,
        out_specs=(done, done),
        compiler_params=params(),
        cost_estimate=cost(8),
        name="combine",
    )(*parts, scale, turn(b), turn(c0), c1)
    whole = (fields, LANE, BAND, LANE)
    return increment.reshape(whole), residual.reshape(whole)


def solution(mesh):
    profile = P(("member", "lon"))
    field = P("member", None, "lon", None)
    return jax.shard_map(
        shards,
        mesh=mesh,
        in_specs=(P("lon", "member"),) + (profile,) * 4 + (P("member", "lon"),) * 2 + (P(),) * 4,
        out_specs=(field, field),
        check_vma=False,
    )
```

```python
import functools

import jax
import jax.numpy as jnp
from jax import lax
from jax.experimental import pallas as pl
from jax.experimental.pallas import tpu as pltpu
from jax.sharding import PartitionSpec as P

F32 = jnp.float32
BF16 = jnp.bfloat16
BAND = 8
LANE = 128
STEPS = 3
PART = 16

NN = (((1,), (0,)), ((), ()))
NT = (((1,), (1,)), ((), ()))


def dot(left, right, dims=NN):
    return lax.dot_general(left, right, dims, preferred_element_type=F32)


def halves(value):
    high = value.astype(BF16)
    return high, (value - high.astype(F32)).astype(BF16)


def thirds(value):
    high = value.astype(BF16)
    rest = value - high.astype(F32)
    middle = rest.astype(BF16)
    return high, middle, (rest - middle.astype(F32)).astype(BF16)


def fold(product):
    return product[:, :LANE] + product[:, LANE:]


def down(row, count):
    return jnp.broadcast_to(row, (LANE, row.shape[1])).T[:, :count]


def pack_kernel(*refs):
    sources, (out, w_rows, d_rows), held = refs[:7], refs[7:10], refs[10:17]
    copies = [
        pltpu.make_async_copy(source, place, refs[17].at[n])
        for n, (source, place) in enumerate(zip(sources, held))
    ]
    for copy in copies:
        copy.start()
    for copy in copies:
        copy.wait()
    owner, lonpos, lat, step, top, innovation, weight = held
    devices, block, _ = out.shape
    count = owner.shape[1]
    slots = w_rows.shape[0]
    cap = slots // devices
    owners = owner[...].astype(F32)
    upright = down(owners, LANE)
    upright = jnp.concatenate([upright] * (count // LANE), axis=1)
    earlier = lax.broadcasted_iota(jnp.int32, (count, count), 0) < lax.broadcasted_iota(
        jnp.int32, (count, count), 1
    )
    same = jnp.where((upright == owners) & earlier, 1.0, 0.0)
    rank = jnp.sum(same, axis=0, keepdims=True)
    slot = (owners * cap + rank).astype(jnp.int32)
    onehot = jnp.where(
        lax.broadcasted_iota(jnp.int32, (slots, count), 0) == slot, 1.0, 0.0
    ).astype(BF16)
    seen = lax.broadcasted_iota(jnp.int32, (LANE, count), 0) < top[...]
    weights = jnp.where(seen, weight[...], 0.0)
    parts = thirds(weights) + thirds(weights * innovation[...])
    rows = dot(onehot, jnp.concatenate(parts, axis=0), NT)
    w_rows[...] = rows[:, 0:128] + rows[:, 128:256] + rows[:, 256:384]
    d_rows[...] = rows[:, 384:512] + rows[:, 512:640] + rows[:, 640:768]
    line = lax.broadcasted_iota(jnp.int32, (8, count), 0)
    facts = jnp.where(
        line == 0, lonpos[...], jnp.where(line == 1, lat[...], jnp.where(line == 2, step[...], 0))
    )
    facts = dot(facts.astype(F32).astype(BF16), onehot, NT)
    first = lax.broadcasted_iota(jnp.int32, (8, LANE), 0) == 0
    inside = lax.broadcasted_iota(jnp.int32, (8, LANE), 1) < cap
    for dest in range(devices):
        out[dest, 0:cap, :] = w_rows[dest * cap : (dest + 1) * cap, :]
        out[dest, cap : 2 * cap, :] = d_rows[dest * cap : (dest + 1) * cap, :]
        at = dest * cap // LANE * LANE
        tile = facts[:, at : at + LANE]
        if dest * cap != at:
            tile = pltpu.roll(tile, LANE - (dest * cap - at), 1)
        column = tile[0:1] * float(LANE) + tile[1:2]
        tile = jnp.where(first, column, tile[2:3])
        out[dest, 2 * cap : 2 * cap + 8, :] = jnp.where(inside, tile, 0.0)


def prepare_kernel(shift, frac, vmix, hcoef, mats, offs, fracs, scale):
    fields = vmix.shape[0]
    for t in range(STEPS):
        offs[t] = shift[t].astype(F32).T
        fracs[t] = frac[t].T
    bound = jnp.zeros((1, 1), F32)
    reach = jnp.zeros((1, LANE), F32)
    for f in range(fields):
        v = vmix[f]
        size = jnp.abs(v)
        over = jnp.max(jnp.sum(size, axis=0, keepdims=True), axis=1, keepdims=True)
        along = jnp.max(jnp.sum(size, axis=1, keepdims=True), axis=0, keepdims=True)
        bound = jnp.maximum(bound, over * along)
        row = hcoef[f : f + 1, :]
        reach = reach + row * row
        turned = v.T
        weighed = turned * row
        for kind, matrix in enumerate((v, weighed.T, turned, weighed)):
            high, low = halves(matrix)
            both = jnp.concatenate([high, low], axis=1)
            mats[kind, f] = jnp.concatenate([both, both], axis=0)
    rho = bound * bound * bound * jnp.max(reach, axis=1, keepdims=True) * 2.0
    rho = jnp.minimum(jnp.maximum(rho, 1e-18), 1e18)
    scale[...] = jnp.broadcast_to(1.0 / rho, (8, LANE))


def place_of(column, step):
    return (step - 1.0) * float(BAND * LANE) + column


def line_of(ref, first, count):
    return jnp.concatenate([ref[first + n : first + n + 1, :] for n in range(count)], axis=1)


def places(ref, slots):
    groups = slots // LANE
    return place_of(line_of(ref, slots, groups), line_of(ref, slots + groups, groups)).astype(
        jnp.int32
    )


def lat_onehot(place, first, count):
    rows = lax.broadcasted_iota(jnp.int32, (count, place.shape[1]), 0) + first
    return jnp.where((place & (LANE - 1)) == rows, 1.0, 0.0).astype(BF16)


def block_mask(place, block, count):
    wide = jnp.broadcast_to(place >> 7, (count, place.shape[1]))
    return jnp.where(wide == block, 1.0, 0.0).astype(BF16)


def edges_of(place, both):
    lats = lat_onehot(place, 0, LANE)
    first = lats * block_mask(place, (STEPS - 1) * BAND, LANE)
    last = lats * block_mask(place, STEPS * BAND - 1, LANE)
    return fold(dot(jnp.concatenate([first, last], axis=0), both))


def unpack_kernel(received, scale, w_out, ex_out, edge_out):
    devices = received.shape[0]
    slots = w_out.shape[0]
    cap = slots // devices
    per = LANE // cap
    groups = slots // LANE
    shrink = scale[0:1, :]
    lines = [jnp.zeros((8, LANE), F32) for _ in range(groups)]
    for source in range(devices):
        at = source * cap
        w_out[at : at + cap, :] = received[source, 0:cap, :] * shrink
        ex_out[at : at + cap, :] = received[source, cap : 2 * cap, :]
        tile = received[source, 2 * cap : 2 * cap + 8, :]
        if source % per:
            tile = pltpu.roll(tile, cap * (source % per), 1)
        lines[source // per] = lines[source // per] + tile
    for n in range(groups):
        ex_out[slots + n : slots + n + 1, :] = lines[n][0:1]
        ex_out[slots + groups + n : slots + groups + n + 1, :] = lines[n][1:2]
    place = places(ex_out, slots)
    both = jnp.concatenate(halves(ex_out[0:slots, :]), axis=1)
    edge_out[...] = edges_of(place, both)


def regions(begin, end):
    return [(begin - t, end + 2 * t) for t in range(1, STEPS + 1)]


def sweep_kernel(full, chunk_size, begin, end, *refs):
    CHUNK = chunk_size
    if full:
        (odd, inner, own, outer, m_inner, m_own, m_outer, e_left, e_right, mats, offs, fracs,
         hcoef, w, _, out, z_out, edge_out, *scratch) = refs
        sel, lats, masks, zs, z1, z2, lz, u, low, ys, reads, third, heard = scratch
    else:
        (odd, inner, own, outer, m_inner, m_own, m_outer, mats, offs, fracs, hcoef, _,
         out, *scratch) = refs
        sel, lats, masks, zs, z1, z2, lz, u, low = scratch
    fields = mats.shape[1]
    slots = zs.shape[1]
    spans = regions(begin, end)
    swapped = odd[0]

    def choose(one, other):
        return jnp.where(jnp.broadcast_to(swapped, one.shape) == 1, one, other)

    near = (inner[0:slots, :], outer[0:slots, :])
    rows_of = (choose(near[0], near[1]), own[0:slots, :], choose(near[1], near[0]))
    near = (places(m_inner, slots), places(m_outer, slots))
    place = (choose(near[0], near[1]), places(m_own, slots), choose(near[1], near[0]))
    blocks = []
    for band in range(3):
        shift = (band - 1) * BAND
        blocks.append(
            [
                (t, i, i + shift - spans[t - 1][0])
                for t in range(1, STEPS + 1)
                for i in range(BAND)
                if spans[t - 1][0] <= i + shift < spans[t - 1][1]
            ]
        )
        high, lo = halves(rows_of[band])
        zs[band, :, 0:LANE] = high
        zs[band, :, LANE:] = lo
        lats[band] = lat_onehot(place[band], 0, LANE)
        for t, i, _ in blocks[band]:
            masks[band, (t - 1) * BAND + i] = block_mask(place[band], (t - 1) * BAND + i, 16)

    wide3 = spans[2][1] - spans[2][0]

    def split_to(ref, at, value):
        high, lo = halves(value)
        ref[at : at + value.shape[0], 0:LANE] = high
        ref[at : at + value.shape[0], LANE:] = lo

    def chunk(c, sums):
        p0 = pl.multiple_of(c * CHUNK, CHUNK)
        here = pl.ds(p0, CHUNK)
        for band in range(3):
            count = len(blocks[band])
            for n, (t, i, _) in enumerate(blocks[band]):
                mask = masks[band, (t - 1) * BAND + i]
                mask = jnp.concatenate([mask] * (CHUNK // 16), axis=0)
                sel[band, n * CHUNK : (n + 1) * CHUNK, :] = lats[band, here, :] * mask
            dense = fold(dot(sel[band, 0 : count * CHUNK, :], zs[band]))
            for n, (t, i, at) in enumerate(blocks[band]):
                slab = dense[n * CHUNK : (n + 1) * CHUNK]
                if t == 3:
                    split_to(lz, at * CHUNK, slab)
                else:
                    (z1 if t == 1 else z2)[at] = slab
        if full:
            split_to(lz, 0, e_left[here, :])
            split_to(lz, (wide3 - 1) * CHUNK, e_right[here, :])

        def advect(f, t, forward, first, last, consume):
            for r in range(0, CHUNK, PART):
                part = slice(r, r + PART)
                a = fracs[t - 1, pl.ds(p0 + r, PART), :]
                s = offs[t - 1, pl.ds(p0 + r, PART), :]
                if forward:
                    s = -s
                back_one = s < 0.0
                same = s == 0.0
                u1, u2 = u[f, first + 1, part], u[f, first + 2, part]
                h = jnp.where(back_one, u[f, first, part], jnp.where(same, u1, u2))
                for j in range(first, last):
                    u3 = u[f, j + 3, part]
                    h2 = jnp.where(back_one, u1, jnp.where(same, u2, u3))
                    if forward:
                        consume(j, r, h2 + a * (h - h2))
                    else:
                        consume(j, r, h + a * (h2 - h))
                    u1, u2, h = u2, u3, h2

        norm = [sums]
        tasks = []

        def stage(kind, wide, source, rest):
            count = max(1, (wide + 4) // 8)
            cuts = [wide * n // count for n in range(count + 1)]
            for f in range(fields):
                for a, b in zip(cuts, cuts[1:]):

                    def multiply(f=f, a=a, b=b):
                        rows = (lz if source is None else source.at[f])[a * CHUNK : b * CHUNK, :]
                        product = fold(dot(rows, mats[kind, f]))
                        u[f, a:b] = product.reshape(b - a, CHUNK, LANE)

                    def follow(f=f, a=a, b=b):
                        rest(f, a, b, max(a - 3, 0), b - 3, b == wide)

                    tasks.append((multiply, follow))

        def adjoint(t, force):
            def rest(f, a, b, first, last, final):
                row = hcoef[f : f + 1, :]

                def keep(j, r, value):
                    value = value + row * force[j, r : r + PART]
                    split_to(low.at[f], j * CHUNK + r, value)

                advect(f, t, False, first, last, keep)

            return rest

        def arrive(f, a, b, first, last, final):
            def keep(j, r, value):
                lon = j + begin
                if full:
                    u[f, j, r : r + PART] = value
                if 0 <= lon < BAND:
                    out[f, lon, pl.ds(p0 + r, PART), :] = value
                    if full:
                        norm[0] = norm[0] + jnp.sum(
                            (value * value).reshape(PART // 8, 8, LANE), axis=0
                        )

            advect(f, 1, False, first, last, keep)
            if full and final:
                leave(1, low.at[f], 0)(f, 0, b - 6)

        def leave(t, target, at):
            def go(f, first, last):
                def keep(j, r, value):
                    high, lo = halves(value)
                    to = slice(j * CHUNK + r, j * CHUNK + r + PART)
                    target[to, at : at + LANE] = high
                    target[to, at + LANE : at + 2 * LANE] = lo

                advect(f, t, True, first, last, keep)

            return go

        def note(t, lon, value):
            high, lo = halves(value)
            to = pl.ds(((t - 1) * BAND + lon) * LANE + p0, CHUNK)
            ys[to, 0:LANE] = high
            ys[to, LANE:] = lo

        def forward(t, begins):
            def rest(f, a, b, first, last, final):
                row = hcoef[f : f + 1, :]
                for lon in range(BAND):
                    if a <= lon - begins < b:
                        term = row * u[f, lon - begins]
                        if f > 0:
                            term = term + heard[lon]
                        if f < fields - 1:
                            heard[lon] = term
                        else:
                            note(t, lon, term)
                if t == 1:
                    leave(2, low.at[f], 0)(f, first, last)
                else:
                    leave(3, third, f * 2 * LANE)(f, first, last)

            return rest

        stage(1, wide3, None, adjoint(3, z2))
        stage(0, wide3 - 3, low, adjoint(2, z1))
        stage(0, wide3 - 6, low, arrive)
        if full:
            stage(2, wide3 - 12, low, forward(1, begin + 2))
            stage(2, wide3 - 15, low, forward(2, begin + 4))
            last_product = []

            def multiply():
                last_product.append(
                    fold(dot(third[...], mats[3].reshape(fields * 2 * LANE, 2 * LANE)))
                )

            def follow():
                for lon in range(BAND):
                    note(3, lon, last_product[0][lon * CHUNK : (lon + 1) * CHUNK])

            tasks.append((lambda: None, lambda: None))
            tasks.append((multiply, follow))
        tasks[0][0]()
        for n in range(len(tasks)):
            if n + 1 < len(tasks):
                tasks[n + 1][0]()
            tasks[n][1]()
        return norm[0]

    sums = lax.fori_loop(0, LANE // CHUNK, chunk, jnp.zeros((8, LANE), F32))
    if not full:
        return

    upright = jnp.concatenate(
        [down(place[1][:, n : n + LANE].astype(F32), LANE) for n in range(0, slots, LANE)], axis=0
    )
    away = upright - lax.broadcasted_iota(jnp.int32, (slots, LANE), 1).astype(F32)
    for block in range(STEPS * BAND):
        reads[:, block * LANE : (block + 1) * LANE] = jnp.where(
            away == float(block * LANE), 1.0, 0.0
        ).astype(BF16)
    y = fold(dot(reads[...], ys[...]))
    z = w[...] * y
    z_out[0:slots, :] = z
    curve = jnp.sum((z * y).reshape(slots // 8, 8, LANE), axis=0)
    edge_out[...] = edges_of(place[1], jnp.concatenate(halves(z), axis=1))
    line = lax.broadcasted_iota(jnp.int32, (8, LANE), 0)
    one = jnp.sum(sums, axis=0, keepdims=True)
    two = jnp.sum(curve, axis=0, keepdims=True)
    z_out[slots : slots + 8, :] = jnp.where(line == 0, one, jnp.where(line == 1, two, 0.0))
    z_out[slots + 2 : slots + 4, :] = own[slots : slots + 2, :]


def turn_kernel(source, out):
    for lon in range(BAND):
        out[0, lon] = source[0, lon].T


def combine_kernel(*refs):
    *moments, scale, b, c0, c1, increment, residual, held, sems = refs
    total = moments[0][...]
    for part in moments[1:]:
        total = total + part[...]
    total = jnp.sum(total, axis=1, keepdims=True)
    base = total[2:3]
    m1 = total[3:4] / base
    m2 = total[0:1] / base
    m3 = total[1:2] / base
    eps = scale[0:1, 0:1]
    ap = 1.0 / (eps + m1)
    alpha = eps * ap
    beta = (m2 - m1 * m1) * ap * ap
    u = 1.0 + beta - alpha
    curve = eps * (u * u - 2.0 * u * ap * m1 + ap * ap * m2) + (
        u * u * m1 - 2.0 * u * ap * m2 + ap * ap * m3
    )
    a2p = beta / curve
    a2 = eps * a2p
    inc_b = alpha + a2 * u
    inc_c = -(a2 * ap)
    res_b = 1.0 - alpha - a2 * u
    res_c = a2 * ap - ap - a2p * u
    res_d = a2p * ap
    copies = []
    for f in range(b.shape[0]):
        for lon in range(BAND):
            b_now, c_now = b[f, lon], c0[f, lon]
            to = pl.ds(lon, LANE, stride=BAND)
            held[0, f, to, :] = inc_b * b_now + inc_c * c_now
            held[1, f, to, :] = res_b * b_now + res_c * c_now + res_d * c1[f, lon].T
        for n, target in enumerate((increment, residual)):
            copy = pltpu.make_async_copy(held.at[n, f], target.at[f], sems.at[n, f])
            copy.start()
            copies.append(copy)
    for copy in copies:
        copy.wait()


def params(mebibytes):
    return pltpu.CompilerParams(vmem_limit_bytes=mebibytes * 1024 * 1024)


def shards(
    obs_owner, obs_lonpos, obs_lat, obs_step, obs_top, innovation, obs_weight,
    wind_shift, wind_frac, vmix, hcoef,
):
    devices = lax.axis_size("lon")
    fields = vmix.shape[0]
    count = obs_owner.shape[0]
    cap = max(2, 2 * count // devices)
    slots = devices * cap
    shape = jax.ShapeDtypeStruct
    state = shape((fields, BAND, LANE, LANE), F32)
    rows = shape((slots, LANE), F32)
    edge = shape((2 * LANE, LANE), F32)
    small = shape((8, LANE), F32)
    more_rows = shape((slots + 8, LANE), F32)

    send = pl.pallas_call(
        pack_kernel,
        out_shape=shape((devices, 2 * cap + 8, LANE), F32),
        in_specs=[pl.BlockSpec(memory_space=pltpu.HBM)] * 7,
        scratch_shapes=[pltpu.VMEM((slots, LANE), F32)] * 2
        + [pltpu.VMEM((1, count), jnp.int32)] * 5
        + [pltpu.VMEM((LANE, count), F32)] * 2
        + [pltpu.SemaphoreType.DMA((7,))],
        compiler_params=params(60),
        name="pack",
    )(
        obs_owner.reshape(1, count), obs_lonpos.reshape(1, count), obs_lat.reshape(1, count),
        obs_step.reshape(1, count), obs_top.reshape(1, count), innovation, obs_weight,
    )
    mats, offs, fracs, scale = pl.pallas_call(
        prepare_kernel,
        out_shape=(
            shape((4, fields, 2 * LANE, 2 * LANE), BF16),
            shape((STEPS, LANE, LANE), F32),
            shape((STEPS, LANE, LANE), F32),
            small,
        ),
        compiler_params=params(16),
        name="prepare",
    )(wind_shift, wind_frac, vmix, hcoef)
    received = lax.all_to_all(send, "lon", split_axis=0, concat_axis=0, tiled=True)
    w, rows_d, edge_d = pl.pallas_call(
        unpack_kernel,
        out_shape=(rows, shape((slots + 8, LANE), F32), edge),
        compiler_params=params(16),
        name="unpack",
    )(received, scale)

    def along(value, hop):
        return lax.ppermute(value, "lon", [(i, (i + hop) % devices) for i in range(devices)])

    def swap(value, first):
        pairs = [((i + first) % devices, (i + 1 + first) % devices) for i in range(0, devices, 2)]
        return lax.ppermute(value, "lon", pairs + [(b, a) for a, b in pairs])

    def near(value):
        return swap(value, 0), value, swap(value, 1)

    def far(edges):
        return along(edges[LANE:], 2), along(edges[:LANE], -2)

    def scratch(full, size, begin, end):
        wide = [b - a for a, b in regions(begin, end)]
        shapes = [
            pltpu.VMEM((3, STEPS * BAND * size, slots), BF16),
            pltpu.VMEM((3, LANE, slots), BF16),
            pltpu.VMEM((3, STEPS * BAND, 16, slots), BF16),
            pltpu.VMEM((3, slots, 2 * LANE), BF16),
            pltpu.VMEM((wide[0], size, LANE), F32),
            pltpu.VMEM((wide[1], size, LANE), F32),
            pltpu.VMEM((wide[2] * size, 2 * LANE), BF16),
            pltpu.VMEM((fields, wide[2], size, LANE), F32),
            pltpu.VMEM((fields, wide[1] * size, 2 * LANE), BF16),
        ]
        if full:
            shapes.append(pltpu.VMEM((STEPS * BAND * LANE, 2 * LANE), BF16))
            shapes.append(pltpu.VMEM((slots, STEPS * BAND * LANE), BF16))
            shapes.append(pltpu.VMEM((BAND * size, fields * 2 * LANE), BF16))
            shapes.append(pltpu.VMEM((BAND, size, LANE), F32))
        return shapes

    def specs(count):
        return [pl.BlockSpec(memory_space=pltpu.SMEM)] + [
            pl.BlockSpec(memory_space=pltpu.VMEM)
        ] * count

    def cost(columns):
        return pl.CostEstimate(
            flops=columns * fields * LANE * 8 * LANE * LANE,
            bytes_accessed=8 * 1024 * 1024,
            transcendentals=0,
        )

    odd = (lax.axis_index("lon") % 2).reshape(1)

    def sweep(rows_near, edges, facts, size, behind):
        return pl.pallas_call(
            functools.partial(sweep_kernel, True, size, -6, BAND + 3),
            out_shape=(state, more_rows, edge),
            in_specs=specs(13) + [pl.BlockSpec(memory_space=pl.ANY)],
            scratch_shapes=scratch(True, size, -6, BAND + 3),
            compiler_params=params(36),
            cost_estimate=cost(130),
            name="sweep",
        )(odd, *rows_near, *facts, *far(edges), mats, offs, fracs, hcoef, w, behind)

    block = pl.BlockSpec((1, BAND, LANE, LANE), lambda f: (f, 0, 0, 0))

    def turn(value):
        return pl.pallas_call(
            turn_kernel,
            out_shape=state,
            grid=(fields,),
            in_specs=[block],
            out_specs=block,
            compiler_params=params(16),
            cost_estimate=cost(8),
            name="turn",
        )(value)

    facts = near(rows_d)
    b, z0, edge0 = sweep(facts, edge_d, facts, 64, scale)
    b = turn(b)
    c0, z1, _ = sweep(near(z0), edge0, facts, 32, b)
    c0 = turn(c0)
    last = near(z1)
    c1 = pl.pallas_call(
        functools.partial(sweep_kernel, False, 32, 0, BAND),
        out_shape=state,
        in_specs=specs(10) + [pl.BlockSpec(memory_space=pl.ANY)],
        scratch_shapes=scratch(False, 32, 0, BAND),
        compiler_params=params(36),
        cost_estimate=cost(60),
        name="last_sweep",
    )(odd, *last, *facts, mats, offs, fracs, hcoef, c0)

    single = z1[slots:]
    window = last[0][slots:] + single + last[2][slots:]
    covered, parts = 3, [window]
    while devices // covered > 1:
        window = functools.reduce(jnp.add, parts)
        count_of = min(devices // covered, 7)
        parts = [window] + [along(window, -k * covered) for k in range(1, count_of)]
        covered = covered * count_of
    parts = parts + [along(single, -(k - 1)) for k in range(covered, devices)]

    flat = shape((fields, LANE * BAND, LANE), F32)
    increment, residual = pl.pallas_call(
        combine_kernel,
        out_shape=(flat, flat),
        in_specs=[pl.BlockSpec(memory_space=pltpu.VMEM)] * (len(parts) + 4),
        out_specs=[pl.BlockSpec(memory_space=pl.ANY)] * 2,
        scratch_shapes=[
            pltpu.VMEM((2, fields, LANE * BAND, LANE), F32),
            pltpu.SemaphoreType.DMA((2, fields)),
        ],
        compiler_params=params(24),
        cost_estimate=cost(8),
        name="combine",
    )(*parts, scale, b, c0, c1)
    whole = (fields, LANE, BAND, LANE)
    return increment.reshape(whole), residual.reshape(whole)


def solution(mesh):
    profile = P(("member", "lon"))
    field = P("member", None, "lon", None)
    return jax.shard_map(
        shards,
        mesh=mesh,
        in_specs=(P("lon", "member"),) + (profile,) * 4 + (P("member", "lon"),) * 2 + (P(),) * 4,
        out_specs=(field, field),
        check_vma=False,
    )
```

```python
import functools

import jax
import jax.numpy as jnp
from jax import lax
from jax.experimental import pallas as pl
from jax.experimental.pallas import tpu as pltpu
from jax.sharding import PartitionSpec as P

F32 = jnp.float32
BF16 = jnp.bfloat16
BAND = 8
LANE = 128
STEPS = 3
PART = 16

NN = (((1,), (0,)), ((), ()))
NT = (((1,), (1,)), ((), ()))


def dot(left, right, dims=NN):
    return lax.dot_general(left, right, dims, preferred_element_type=F32)


def halves(value):
    high = value.astype(BF16)
    return high, (value - high.astype(F32)).astype(BF16)


def thirds(value):
    high = value.astype(BF16)
    rest = value - high.astype(F32)
    middle = rest.astype(BF16)
    return high, middle, (rest - middle.astype(F32)).astype(BF16)


def fold(product):
    return product[:, :LANE] + product[:, LANE:]


def down(row, count):
    return jnp.broadcast_to(row, (LANE, row.shape[1])).T[:, :count]


def pack_kernel(*refs):
    sources, (out, w_rows, d_rows), held = refs[:7], refs[7:10], refs[10:17]
    copies = [
        pltpu.make_async_copy(source, place, refs[17].at[n])
        for n, (source, place) in enumerate(zip(sources, held))
    ]
    for copy in copies:
        copy.start()
    for copy in copies:
        copy.wait()
    owner, lonpos, lat, step, top, innovation, weight = held
    devices, block, _ = out.shape
    count = owner.shape[1]
    slots = w_rows.shape[0]
    cap = slots // devices
    owners = owner[...].astype(F32)
    upright = down(owners, LANE)
    upright = jnp.concatenate([upright] * (count // LANE), axis=1)
    earlier = lax.broadcasted_iota(jnp.int32, (count, count), 0) < lax.broadcasted_iota(
        jnp.int32, (count, count), 1
    )
    same = jnp.where((upright == owners) & earlier, 1.0, 0.0)
    rank = jnp.sum(same, axis=0, keepdims=True)
    slot = (owners * cap + rank).astype(jnp.int32)
    onehot = jnp.where(
        lax.broadcasted_iota(jnp.int32, (slots, count), 0) == slot, 1.0, 0.0
    ).astype(BF16)
    seen = lax.broadcasted_iota(jnp.int32, (LANE, count), 0) < top[...]
    weights = jnp.where(seen, weight[...], 0.0)
    parts = thirds(weights) + thirds(weights * innovation[...])
    rows = dot(onehot, jnp.concatenate(parts, axis=0), NT)
    w_rows[...] = rows[:, 0:128] + rows[:, 128:256] + rows[:, 256:384]
    d_rows[...] = rows[:, 384:512] + rows[:, 512:640] + rows[:, 640:768]
    line = lax.broadcasted_iota(jnp.int32, (8, count), 0)
    facts = jnp.where(
        line == 0, lonpos[...], jnp.where(line == 1, lat[...], jnp.where(line == 2, step[...], 0))
    )
    facts = dot(facts.astype(F32).astype(BF16), onehot, NT)
    first = lax.broadcasted_iota(jnp.int32, (8, LANE), 0) == 0
    inside = lax.broadcasted_iota(jnp.int32, (8, LANE), 1) < cap
    for dest in range(devices):
        out[dest, 0:cap, :] = w_rows[dest * cap : (dest + 1) * cap, :]
        out[dest, cap : 2 * cap, :] = d_rows[dest * cap : (dest + 1) * cap, :]
        at = dest * cap // LANE * LANE
        tile = facts[:, at : at + LANE]
        if dest * cap != at:
            tile = pltpu.roll(tile, LANE - (dest * cap - at), 1)
        column = tile[0:1] * float(LANE) + tile[1:2]
        tile = jnp.where(first, column, tile[2:3])
        out[dest, 2 * cap : 2 * cap + 8, :] = jnp.where(inside, tile, 0.0)


def prepare_kernel(shift, frac, vmix, hcoef, mats, offs, fracs, scale):
    fields = vmix.shape[0]
    for t in range(STEPS):
        offs[t] = shift[t].astype(F32).T
        fracs[t] = frac[t].T
    bound = jnp.zeros((1, 1), F32)
    reach = jnp.zeros((1, LANE), F32)
    for f in range(fields):
        v = vmix[f]
        size = jnp.abs(v)
        over = jnp.max(jnp.sum(size, axis=0, keepdims=True), axis=1, keepdims=True)
        along = jnp.max(jnp.sum(size, axis=1, keepdims=True), axis=0, keepdims=True)
        bound = jnp.maximum(bound, over * along)
        row = hcoef[f : f + 1, :]
        reach = reach + row * row
        turned = v.T
        weighed = turned * row
        for kind, matrix in enumerate((v, weighed.T, turned, weighed)):
            high, low = halves(matrix)
            both = jnp.concatenate([high, low], axis=1)
            mats[kind, f] = jnp.concatenate([both, both], axis=0)
    rho = bound * bound * bound * jnp.max(reach, axis=1, keepdims=True) * 2.0
    rho = jnp.minimum(jnp.maximum(rho, 1e-18), 1e18)
    scale[...] = jnp.broadcast_to(1.0 / rho, (8, LANE))


def place_of(column, step):
    return (step - 1.0) * float(BAND * LANE) + column


def line_of(ref, first, count):
    return jnp.concatenate([ref[first + n : first + n + 1, :] for n in range(count)], axis=1)


def places(ref, slots):
    groups = slots // LANE
    return place_of(line_of(ref, slots, groups), line_of(ref, slots + groups, groups)).astype(
        jnp.int32
    )


def lat_onehot(place, first, count):
    rows = lax.broadcasted_iota(jnp.int32, (count, place.shape[1]), 0) + first
    return jnp.where((place & (LANE - 1)) == rows, 1.0, 0.0).astype(BF16)


def block_mask(place, block, count):
    wide = jnp.broadcast_to(place >> 7, (count, place.shape[1]))
    return jnp.where(wide == block, 1.0, 0.0).astype(BF16)


def edges_of(place, both):
    lats = lat_onehot(place, 0, LANE)
    first = lats * block_mask(place, (STEPS - 1) * BAND, LANE)
    last = lats * block_mask(place, STEPS * BAND - 1, LANE)
    return fold(dot(jnp.concatenate([first, last], axis=0), both))


def unpack_kernel(received, scale, w_out, ex_out, edge_out):
    devices = received.shape[0]
    slots = w_out.shape[0]
    cap = slots // devices
    per = LANE // cap
    groups = slots // LANE
    shrink = scale[0:1, :]
    lines = [jnp.zeros((8, LANE), F32) for _ in range(groups)]
    for source in range(devices):
        at = source * cap
        w_out[at : at + cap, :] = received[source, 0:cap, :] * shrink
        ex_out[at : at + cap, :] = received[source, cap : 2 * cap, :]
        tile = received[source, 2 * cap : 2 * cap + 8, :]
        if source % per:
            tile = pltpu.roll(tile, cap * (source % per), 1)
        lines[source // per] = lines[source // per] + tile
    for n in range(groups):
        ex_out[slots + n : slots + n + 1, :] = lines[n][0:1]
        ex_out[slots + groups + n : slots + groups + n + 1, :] = lines[n][1:2]
    place = places(ex_out, slots)
    both = jnp.concatenate(halves(ex_out[0:slots, :]), axis=1)
    edge_out[...] = edges_of(place, both)


def regions(begin, end):
    return [(begin - t, end + 2 * t) for t in range(1, STEPS + 1)]


def sweep_kernel(full, chunk_size, batch, begin, end, *refs):
    CHUNK = chunk_size
    if full:
        (odd, inner, own, outer, m_inner, m_own, m_outer, e_left, e_right, mats, offs, fracs,
         hcoef, w, _, out, z_out, edge_out, *scratch) = refs
        sel, lats, masks, zs, z1, z2, lz, u, low, ys, reads, third, heard = scratch
    else:
        (odd, inner, own, outer, m_inner, m_own, m_outer, mats, offs, fracs, hcoef, _,
         out, *scratch) = refs
        sel, lats, masks, zs, z1, z2, lz, u, low = scratch
    fields = mats.shape[1]
    slots = zs.shape[1]
    spans = regions(begin, end)
    swapped = odd[0]

    def choose(one, other):
        return jnp.where(jnp.broadcast_to(swapped, one.shape) == 1, one, other)

    near = (inner[0:slots, :], outer[0:slots, :])
    rows_of = (choose(near[0], near[1]), own[0:slots, :], choose(near[1], near[0]))
    near = (places(m_inner, slots), places(m_outer, slots))
    place = (choose(near[0], near[1]), places(m_own, slots), choose(near[1], near[0]))
    blocks = []
    for band in range(3):
        shift = (band - 1) * BAND
        blocks.append(
            [
                (t, i, i + shift - spans[t - 1][0])
                for t in range(1, STEPS + 1)
                for i in range(BAND)
                if spans[t - 1][0] <= i + shift < spans[t - 1][1]
            ]
        )
        high, lo = halves(rows_of[band])
        zs[band, :, 0:LANE] = high
        zs[band, :, LANE:] = lo
        lats[band] = lat_onehot(place[band], 0, LANE)
        for t, i, _ in blocks[band]:
            masks[band, (t - 1) * BAND + i] = block_mask(place[band], (t - 1) * BAND + i, 16)

    wide3 = spans[2][1] - spans[2][0]

    def split_to(ref, at, value):
        high, lo = halves(value)
        ref[at : at + value.shape[0], 0:LANE] = high
        ref[at : at + value.shape[0], LANE:] = lo

    def chunk(c, sums):
        p0 = pl.multiple_of(c * CHUNK, CHUNK)
        here = pl.ds(p0, CHUNK)
        for band in range(3):
            count = len(blocks[band])
            for n, (t, i, _) in enumerate(blocks[band]):
                mask = masks[band, (t - 1) * BAND + i]
                mask = jnp.concatenate([mask] * (CHUNK // 16), axis=0)
                sel[band, n * CHUNK : (n + 1) * CHUNK, :] = lats[band, here, :] * mask
            dense = fold(dot(sel[band, 0 : count * CHUNK, :], zs[band]))
            for n, (t, i, at) in enumerate(blocks[band]):
                slab = dense[n * CHUNK : (n + 1) * CHUNK]
                if t == 3:
                    split_to(lz, at * CHUNK, slab)
                else:
                    (z1 if t == 1 else z2)[at] = slab
        if full:
            split_to(lz, 0, e_left[here, :])
            split_to(lz, (wide3 - 1) * CHUNK, e_right[here, :])

        def advect(f, t, forward, first, last, consume):
            for r in range(0, CHUNK, PART):
                part = slice(r, r + PART)
                a = fracs[t - 1, pl.ds(p0 + r, PART), :]
                s = offs[t - 1, pl.ds(p0 + r, PART), :]
                if forward:
                    s = -s
                back_one = s < 0.0
                same = s == 0.0
                u1, u2 = u[f, first + 1, part], u[f, first + 2, part]
                h = jnp.where(back_one, u[f, first, part], jnp.where(same, u1, u2))
                for j in range(first, last):
                    u3 = u[f, j + 3, part]
                    h2 = jnp.where(back_one, u1, jnp.where(same, u2, u3))
                    if forward:
                        consume(j, r, h2 + a * (h - h2))
                    else:
                        consume(j, r, h + a * (h2 - h))
                    u1, u2, h = u2, u3, h2

        def sweep_fields(base, sums):
            norm = [sums]
            tasks = []

            def stage(kind, wide, source, rest):
                for f in range(batch):

                    def multiply(f=f):
                        rows = (lz if source is None else source.at[f])[0 : wide * CHUNK, :]
                        product = fold(dot(rows, mats[kind, base + f]))
                        u[f, 0:wide] = product.reshape(wide, CHUNK, LANE)

                    def follow(f=f):
                        rest(f, wide)

                    tasks.append((multiply, follow))

            def row_of(f):
                return hcoef[pl.ds(base + f, 1), :]

            def adjoint(t, force):
                def rest(f, wide):
                    row = row_of(f)

                    def keep(j, r, value):
                        value = value + row * force[j, r : r + PART]
                        split_to(low.at[f], j * CHUNK + r, value)

                    advect(f, t, False, 0, wide - 3, keep)

                return rest

            def leave(t, f, target, wide):
                def keep(j, r, value):
                    split_to(target, j * CHUNK + r, value)

                advect(f, t, True, 0, wide - 3, keep)

            def arrive(f, wide):
                def keep(j, r, value):
                    lon = j + begin
                    if full:
                        u[f, j, r : r + PART] = value
                    if 0 <= lon < BAND:
                        out[base + f, lon, pl.ds(p0 + r, PART), :] = value
                        if full:
                            norm[0] = norm[0] + jnp.sum(
                                (value * value).reshape(PART // 8, 8, LANE), axis=0
                            )

                advect(f, 1, False, 0, wide - 3, keep)
                if full:
                    leave(1, f, low.at[f], wide - 3)

            def forward(t, begins):
                def rest(f, wide):
                    row = row_of(f)
                    for lon in range(BAND):
                        heard[t - 1, lon] = heard[t - 1, lon] + row * u[f, lon - begins]
                    leave(t + 1, f, low.at[f] if t == 1 else third.at[base + f], wide)

                return rest

            stage(1, wide3, None, adjoint(3, z2))
            stage(0, wide3 - 3, low, adjoint(2, z1))
            stage(0, wide3 - 6, low, arrive)
            if full:
                stage(2, wide3 - 12, low, forward(1, begin + 2))
                stage(2, wide3 - 15, low, forward(2, begin + 4))
            if batch == 1:
                for multiply, follow in tasks:
                    multiply()
                    follow()
            else:
                tasks[0][0]()
                for n in range(len(tasks)):
                    if n + 1 < len(tasks):
                        tasks[n + 1][0]()
                    tasks[n][1]()
            return norm[0]

        if full:
            heard[...] = jnp.zeros(heard.shape, F32)
        if batch == fields:
            sums = sweep_fields(0, sums)
        else:
            sums = lax.fori_loop(
                0, fields // batch, lambda n, total: sweep_fields(n * batch, total), sums
            )
        if full:
            total = dot(third[0], mats[3, 0])
            for f in range(1, fields):
                total = total + dot(third[f], mats[3, f])
            total = fold(total)
            for t in (1, 2, 3):
                for lon in range(BAND):
                    if t < 3:
                        value = heard[t - 1, lon]
                    else:
                        value = total[lon * CHUNK : (lon + 1) * CHUNK]
                    high, lo = halves(value)
                    to = pl.ds(((t - 1) * BAND + lon) * LANE + p0, CHUNK)
                    ys[to, 0:LANE] = high
                    ys[to, LANE:] = lo
        return sums

    sums = lax.fori_loop(0, LANE // CHUNK, chunk, jnp.zeros((8, LANE), F32))
    if not full:
        return

    upright = jnp.concatenate(
        [down(place[1][:, n : n + LANE].astype(F32), LANE) for n in range(0, slots, LANE)], axis=0
    )
    away = upright - lax.broadcasted_iota(jnp.int32, (slots, LANE), 1).astype(F32)
    for block in range(STEPS * BAND):
        reads[:, block * LANE : (block + 1) * LANE] = jnp.where(
            away == float(block * LANE), 1.0, 0.0
        ).astype(BF16)
    y = fold(dot(reads[...], ys[...]))
    z = w[...] * y
    z_out[0:slots, :] = z
    curve = jnp.sum((z * y).reshape(slots // 8, 8, LANE), axis=0)
    edge_out[...] = edges_of(place[1], jnp.concatenate(halves(z), axis=1))
    line = lax.broadcasted_iota(jnp.int32, (8, LANE), 0)
    one = jnp.sum(sums, axis=0, keepdims=True)
    two = jnp.sum(curve, axis=0, keepdims=True)
    z_out[slots : slots + 8, :] = jnp.where(line == 0, one, jnp.where(line == 1, two, 0.0))
    z_out[slots + 2 : slots + 4, :] = own[slots : slots + 2, :]


def turn_kernel(source, out):
    for lon in range(BAND):
        out[0, lon] = source[0, lon].T


def combine_kernel(*refs):
    *moments, scale, b, c0, c1, increment, residual, held, sems = refs
    total = moments[0][...]
    for part in moments[1:]:
        total = total + part[...]
    total = jnp.sum(total, axis=1, keepdims=True)
    base = total[2:3]
    m1 = total[3:4] / base
    m2 = total[0:1] / base
    m3 = total[1:2] / base
    eps = scale[0:1, 0:1]
    ap = 1.0 / (eps + m1)
    alpha = eps * ap
    beta = (m2 - m1 * m1) * ap * ap
    u = 1.0 + beta - alpha
    curve = eps * (u * u - 2.0 * u * ap * m1 + ap * ap * m2) + (
        u * u * m1 - 2.0 * u * ap * m2 + ap * ap * m3
    )
    a2p = beta / curve
    a2 = eps * a2p
    inc_b = alpha + a2 * u
    inc_c = -(a2 * ap)
    res_b = 1.0 - alpha - a2 * u
    res_c = a2 * ap - ap - a2p * u
    res_d = a2p * ap
    copies = []
    for f in range(b.shape[0]):
        for lon in range(BAND):
            b_now, c_now = b[f, lon], c0[f, lon]
            to = pl.ds(lon, LANE, stride=BAND)
            held[0, f, to, :] = inc_b * b_now + inc_c * c_now
            held[1, f, to, :] = res_b * b_now + res_c * c_now + res_d * c1[f, lon].T
        for n, target in enumerate((increment, residual)):
            copy = pltpu.make_async_copy(held.at[n, f], target.at[f], sems.at[n, f])
            copy.start()
            copies.append(copy)
    for copy in copies:
        copy.wait()


def params(mebibytes):
    return pltpu.CompilerParams(vmem_limit_bytes=mebibytes * 1024 * 1024)


def shards(
    obs_owner, obs_lonpos, obs_lat, obs_step, obs_top, innovation, obs_weight,
    wind_shift, wind_frac, vmix, hcoef,
):
    devices = lax.axis_size("lon")
    fields = vmix.shape[0]
    count = obs_owner.shape[0]
    cap = max(2, 2 * count // devices)
    slots = devices * cap
    shape = jax.ShapeDtypeStruct
    state = shape((fields, BAND, LANE, LANE), F32)
    rows = shape((slots, LANE), F32)
    edge = shape((2 * LANE, LANE), F32)
    small = shape((8, LANE), F32)
    more_rows = shape((slots + 8, LANE), F32)

    send = pl.pallas_call(
        pack_kernel,
        out_shape=shape((devices, 2 * cap + 8, LANE), F32),
        in_specs=[pl.BlockSpec(memory_space=pltpu.HBM)] * 7,
        scratch_shapes=[pltpu.VMEM((slots, LANE), F32)] * 2
        + [pltpu.VMEM((1, count), jnp.int32)] * 5
        + [pltpu.VMEM((LANE, count), F32)] * 2
        + [pltpu.SemaphoreType.DMA((7,))],
        compiler_params=params(60),
        name="pack",
    )(
        obs_owner.reshape(1, count), obs_lonpos.reshape(1, count), obs_lat.reshape(1, count),
        obs_step.reshape(1, count), obs_top.reshape(1, count), innovation, obs_weight,
    )
    mats, offs, fracs, scale = pl.pallas_call(
        prepare_kernel,
        out_shape=(
            shape((4, fields, 2 * LANE, 2 * LANE), BF16),
            shape((STEPS, LANE, LANE), F32),
            shape((STEPS, LANE, LANE), F32),
            small,
        ),
        compiler_params=params(28),
        name="prepare",
    )(wind_shift, wind_frac, vmix, hcoef)
    received = lax.all_to_all(send, "lon", split_axis=0, concat_axis=0, tiled=True)
    w, rows_d, edge_d = pl.pallas_call(
        unpack_kernel,
        out_shape=(rows, shape((slots + 8, LANE), F32), edge),
        compiler_params=params(28),
        name="unpack",
    )(received, scale)

    def along(value, hop):
        return lax.ppermute(value, "lon", [(i, (i + hop) % devices) for i in range(devices)])

    def swap(value, first):
        pairs = [((i + first) % devices, (i + 1 + first) % devices) for i in range(0, devices, 2)]
        return lax.ppermute(value, "lon", pairs + [(b, a) for a, b in pairs])

    def near(value):
        return swap(value, 0), value, swap(value, 1)

    def far(edges):
        return along(edges[LANE:], 2), along(edges[:LANE], -2)

    def scratch(full, size, batch, begin, end):
        wide = [b - a for a, b in regions(begin, end)]
        shapes = [
            pltpu.VMEM((3, STEPS * BAND * size, slots), BF16),
            pltpu.VMEM((3, LANE, slots), BF16),
            pltpu.VMEM((3, STEPS * BAND, 16, slots), BF16),
            pltpu.VMEM((3, slots, 2 * LANE), BF16),
            pltpu.VMEM((wide[0], size, LANE), F32),
            pltpu.VMEM((wide[1], size, LANE), F32),
            pltpu.VMEM((wide[2] * size, 2 * LANE), BF16),
            pltpu.VMEM((batch, wide[2], size, LANE), F32),
            pltpu.VMEM((batch, wide[1] * size, 2 * LANE), BF16),
        ]
        if full:
            shapes.append(pltpu.VMEM((STEPS * BAND * LANE, 2 * LANE), BF16))
            shapes.append(pltpu.VMEM((slots, STEPS * BAND * LANE), BF16))
            shapes.append(pltpu.VMEM((fields, BAND * size, 2 * LANE), BF16))
            shapes.append(pltpu.VMEM((2, BAND, size, LANE), F32))
        return shapes

    def specs(count):
        return [pl.BlockSpec(memory_space=pltpu.SMEM)] + [
            pl.BlockSpec(memory_space=pltpu.VMEM)
        ] * count

    def cost(columns):
        return pl.CostEstimate(
            flops=columns * fields * LANE * 8 * LANE * LANE,
            bytes_accessed=8 * 1024 * 1024,
            transcendentals=0,
        )

    odd = (lax.axis_index("lon") % 2).reshape(1)

    def sweep(rows_near, edges, facts, size, batch, behind):
        return pl.pallas_call(
            functools.partial(sweep_kernel, True, size, batch, -6, BAND + 3),
            out_shape=(state, more_rows, edge),
            in_specs=specs(13) + [pl.BlockSpec(memory_space=pl.ANY)],
            scratch_shapes=scratch(True, size, batch, -6, BAND + 3),
            compiler_params=params(28),
            cost_estimate=cost(130),
            name="sweep",
        )(odd, *rows_near, *facts, *far(edges), mats, offs, fracs, hcoef, w, behind)

    block = pl.BlockSpec((1, BAND, LANE, LANE), lambda f: (f, 0, 0, 0))

    def turn(value):
        return pl.pallas_call(
            turn_kernel,
            out_shape=state,
            grid=(fields,),
            in_specs=[block],
            out_specs=block,
            compiler_params=params(28),
            cost_estimate=cost(8),
            name="turn",
        )(value)

    facts = near(rows_d)
    b, z0, edge0 = sweep(facts, edge_d, facts, 32, fields, scale)
    b = turn(b)
    c0, z1, _ = sweep(near(z0), edge0, facts, 32, 2, b)
    c0 = turn(c0)
    last = near(z1)
    c1 = pl.pallas_call(
        functools.partial(sweep_kernel, False, 64, 1, 0, BAND),
        out_shape=state,
        in_specs=specs(10) + [pl.BlockSpec(memory_space=pl.ANY)],
        scratch_shapes=scratch(False, 64, 1, 0, BAND),
        compiler_params=params(28),
        cost_estimate=cost(60),
        name="last_sweep",
    )(odd, *last, *facts, mats, offs, fracs, hcoef, c0)

    single = z1[slots:]
    window = last[0][slots:] + single + last[2][slots:]
    covered, parts = 3, [window]
    while devices // covered > 1:
        window = functools.reduce(jnp.add, parts)
        count_of = min(devices // covered, 7)
        parts = [window] + [along(window, -k * covered) for k in range(1, count_of)]
        covered = covered * count_of
    parts = parts + [along(single, -(k - 1)) for k in range(covered, devices)]

    flat = shape((fields, LANE * BAND, LANE), F32)
    increment, residual = pl.pallas_call(
        combine_kernel,
        out_shape=(flat, flat),
        in_specs=[pl.BlockSpec(memory_space=pltpu.VMEM)] * (len(parts) + 4),
        out_specs=[pl.BlockSpec(memory_space=pl.ANY)] * 2,
        scratch_shapes=[
            pltpu.VMEM((2, fields, LANE * BAND, LANE), F32),
            pltpu.SemaphoreType.DMA((2, fields)),
        ],
        compiler_params=params(28),
        cost_estimate=cost(8),
        name="combine",
    )(*parts, scale, b, c0, c1)
    whole = (fields, LANE, BAND, LANE)
    return increment.reshape(whole), residual.reshape(whole)


def solution(mesh):
    profile = P(("member", "lon"))
    field = P("member", None, "lon", None)
    return jax.shard_map(
        shards,
        mesh=mesh,
        in_specs=(P("lon", "member"),) + (profile,) * 4 + (P("member", "lon"),) * 2 + (P(),) * 4,
        out_specs=(field, field),
        check_vma=False,
    )
```

```python
import functools

import jax
import jax.numpy as jnp
from jax import lax
from jax.experimental import pallas as pl
from jax.experimental.pallas import tpu as pltpu
from jax.sharding import PartitionSpec as P

F32 = jnp.float32
BF16 = jnp.bfloat16
BAND = 8
LANE = 128
STEPS = 3
PART = 16

NN = (((1,), (0,)), ((), ()))
NT = (((1,), (1,)), ((), ()))


def dot(left, right, dims=NN):
    return lax.dot_general(left, right, dims, preferred_element_type=F32)


def halves(value):
    high = value.astype(BF16)
    return high, (value - high.astype(F32)).astype(BF16)


def thirds(value):
    high = value.astype(BF16)
    rest = value - high.astype(F32)
    middle = rest.astype(BF16)
    return high, middle, (rest - middle.astype(F32)).astype(BF16)


def fold(product):
    return product[:, :LANE] + product[:, LANE:]


def down(row, count):
    return jnp.broadcast_to(row, (LANE, row.shape[1])).T[:, :count]


def pack_kernel(*refs):
    sources, (out, w_rows, d_rows), held = refs[:7], refs[7:10], refs[10:17]
    copies = [
        pltpu.make_async_copy(source, place, refs[17].at[n])
        for n, (source, place) in enumerate(zip(sources, held))
    ]
    for copy in copies:
        copy.start()
    for copy in copies:
        copy.wait()
    owner, lonpos, lat, step, top, innovation, weight = held
    devices, block, _ = out.shape
    count = owner.shape[1]
    slots = w_rows.shape[0]
    cap = slots // devices
    owners = owner[...].astype(F32)
    upright = down(owners, LANE)
    upright = jnp.concatenate([upright] * (count // LANE), axis=1)
    earlier = lax.broadcasted_iota(jnp.int32, (count, count), 0) < lax.broadcasted_iota(
        jnp.int32, (count, count), 1
    )
    same = jnp.where((upright == owners) & earlier, 1.0, 0.0)
    rank = jnp.sum(same, axis=0, keepdims=True)
    slot = (owners * cap + rank).astype(jnp.int32)
    onehot = jnp.where(
        lax.broadcasted_iota(jnp.int32, (slots, count), 0) == slot, 1.0, 0.0
    ).astype(BF16)
    seen = lax.broadcasted_iota(jnp.int32, (LANE, count), 0) < top[...]
    weights = jnp.where(seen, weight[...], 0.0)
    parts = thirds(weights) + thirds(weights * innovation[...])
    rows = dot(onehot, jnp.concatenate(parts, axis=0), NT)
    w_rows[...] = rows[:, 0:128] + rows[:, 128:256] + rows[:, 256:384]
    d_rows[...] = rows[:, 384:512] + rows[:, 512:640] + rows[:, 640:768]
    line = lax.broadcasted_iota(jnp.int32, (8, count), 0)
    facts = jnp.where(
        line == 0, lonpos[...], jnp.where(line == 1, lat[...], jnp.where(line == 2, step[...], 0))
    )
    facts = dot(facts.astype(F32).astype(BF16), onehot, NT)
    first = lax.broadcasted_iota(jnp.int32, (8, LANE), 0) == 0
    inside = lax.broadcasted_iota(jnp.int32, (8, LANE), 1) < cap
    for dest in range(devices):
        out[dest, 0:cap, :] = w_rows[dest * cap : (dest + 1) * cap, :]
        out[dest, cap : 2 * cap, :] = d_rows[dest * cap : (dest + 1) * cap, :]
        at = dest * cap // LANE * LANE
        tile = facts[:, at : at + LANE]
        if dest * cap != at:
            tile = pltpu.roll(tile, LANE - (dest * cap - at), 1)
        column = tile[0:1] * float(LANE) + tile[1:2]
        tile = jnp.where(first, column, tile[2:3])
        out[dest, 2 * cap : 2 * cap + 8, :] = jnp.where(inside, tile, 0.0)


def prepare_kernel(shift, frac, vmix, hcoef, mats, offs, fracs, scale):
    fields = vmix.shape[0]
    for t in range(STEPS):
        offs[t] = shift[t].astype(F32).T
        fracs[t] = frac[t].T
    bound = jnp.zeros((1, 1), F32)
    reach = jnp.zeros((1, LANE), F32)
    for f in range(fields):
        v = vmix[f]
        size = jnp.abs(v)
        over = jnp.max(jnp.sum(size, axis=0, keepdims=True), axis=1, keepdims=True)
        along = jnp.max(jnp.sum(size, axis=1, keepdims=True), axis=0, keepdims=True)
        bound = jnp.maximum(bound, over * along)
        row = hcoef[f : f + 1, :]
        reach = reach + row * row
        turned = v.T
        weighed = turned * row
        for kind, matrix in enumerate((v, weighed.T, turned, weighed)):
            high, low = halves(matrix)
            both = jnp.concatenate([high, low], axis=1)
            mats[kind, f] = jnp.concatenate([both, both], axis=0)
    rho = bound * bound * bound * jnp.max(reach, axis=1, keepdims=True) * 2.0
    rho = jnp.minimum(jnp.maximum(rho, 1e-18), 1e18)
    scale[...] = jnp.broadcast_to(1.0 / rho, (8, LANE))


def place_of(column, step):
    return (step - 1.0) * float(BAND * LANE) + column


def line_of(ref, first, count):
    return jnp.concatenate([ref[first + n : first + n + 1, :] for n in range(count)], axis=1)


def places(ref, slots):
    groups = slots // LANE
    return place_of(line_of(ref, slots, groups), line_of(ref, slots + groups, groups)).astype(
        jnp.int32
    )


def lat_onehot(place, first, count):
    rows = lax.broadcasted_iota(jnp.int32, (count, place.shape[1]), 0) + first
    return jnp.where((place & (LANE - 1)) == rows, 1.0, 0.0).astype(BF16)


def block_mask(place, block, count):
    wide = jnp.broadcast_to(place >> 7, (count, place.shape[1]))
    return jnp.where(wide == block, 1.0, 0.0).astype(BF16)


def edges_of(place, both):
    lats = lat_onehot(place, 0, LANE)
    first = lats * block_mask(place, (STEPS - 1) * BAND, LANE)
    last = lats * block_mask(place, STEPS * BAND - 1, LANE)
    return fold(dot(jnp.concatenate([first, last], axis=0), both))


def unpack_kernel(received, scale, w_out, ex_out, edge_out):
    devices = received.shape[0]
    slots = w_out.shape[0]
    cap = slots // devices
    per = LANE // cap
    groups = slots // LANE
    shrink = scale[0:1, :]
    lines = [jnp.zeros((8, LANE), F32) for _ in range(groups)]
    for source in range(devices):
        at = source * cap
        w_out[at : at + cap, :] = received[source, 0:cap, :] * shrink
        ex_out[at : at + cap, :] = received[source, cap : 2 * cap, :]
        tile = received[source, 2 * cap : 2 * cap + 8, :]
        if source % per:
            tile = pltpu.roll(tile, cap * (source % per), 1)
        lines[source // per] = lines[source // per] + tile
    for n in range(groups):
        ex_out[slots + n : slots + n + 1, :] = lines[n][0:1]
        ex_out[slots + groups + n : slots + groups + n + 1, :] = lines[n][1:2]
    place = places(ex_out, slots)
    both = jnp.concatenate(halves(ex_out[0:slots, :]), axis=1)
    edge_out[...] = edges_of(place, both)


def regions(begin, end):
    return [(begin - t, end + 2 * t) for t in range(1, STEPS + 1)]


def sweep_kernel(full, chunk_size, batch, begin, end, *refs):
    CHUNK = chunk_size
    if full:
        (odd, inner, own, outer, m_inner, m_own, m_outer, e_left, e_right, mats, offs, fracs,
         hcoef, w, _, out, z_out, edge_out, *scratch) = refs
        sel, lats, masks, zs, z1, z2, lz, u, low, ys, reads, third, heard = scratch
    else:
        (odd, inner, own, outer, m_inner, m_own, m_outer, mats, offs, fracs, hcoef, _,
         out, *scratch) = refs
        sel, lats, masks, zs, z1, z2, lz, u, low = scratch
    fields = mats.shape[1]
    slots = zs.shape[1]
    spans = regions(begin, end)
    swapped = odd[0]

    def choose(one, other):
        return jnp.where(jnp.broadcast_to(swapped, one.shape) == 1, one, other)

    near = (inner[0:slots, :], outer[0:slots, :])
    rows_of = (choose(near[0], near[1]), own[0:slots, :], choose(near[1], near[0]))
    near = (places(m_inner, slots), places(m_outer, slots))
    place = (choose(near[0], near[1]), places(m_own, slots), choose(near[1], near[0]))
    blocks = []
    for band in range(3):
        shift = (band - 1) * BAND
        blocks.append(
            [
                (t, i, i + shift - spans[t - 1][0])
                for t in range(1, STEPS + 1)
                for i in range(BAND)
                if spans[t - 1][0] <= i + shift < spans[t - 1][1]
            ]
        )
        high, lo = halves(rows_of[band])
        zs[band, :, 0:LANE] = high
        zs[band, :, LANE:] = lo
        lats[band] = lat_onehot(place[band], 0, LANE)
        for t, i, _ in blocks[band]:
            masks[band, (t - 1) * BAND + i] = block_mask(place[band], (t - 1) * BAND + i, 16)

    wide3 = spans[2][1] - spans[2][0]

    def split_to(ref, at, value):
        high, lo = halves(value)
        ref[at : at + value.shape[0], 0:LANE] = high
        ref[at : at + value.shape[0], LANE:] = lo

    def chunk(c, sums):
        p0 = pl.multiple_of(c * CHUNK, CHUNK)
        here = pl.ds(p0, CHUNK)
        for band in range(3):
            count = len(blocks[band])
            for n, (t, i, _) in enumerate(blocks[band]):
                mask = masks[band, (t - 1) * BAND + i]
                mask = jnp.concatenate([mask] * (CHUNK // 16), axis=0)
                sel[band, n * CHUNK : (n + 1) * CHUNK, :] = lats[band, here, :] * mask
            dense = fold(dot(sel[band, 0 : count * CHUNK, :], zs[band]))
            for n, (t, i, at) in enumerate(blocks[band]):
                slab = dense[n * CHUNK : (n + 1) * CHUNK]
                if t == 3:
                    split_to(lz, at * CHUNK, slab)
                else:
                    (z1 if t == 1 else z2)[at] = slab
        if full:
            split_to(lz, 0, e_left[here, :])
            split_to(lz, (wide3 - 1) * CHUNK, e_right[here, :])

        def advect(f, t, forward, first, last, consume):
            for r in range(0, CHUNK, PART):
                part = slice(r, r + PART)
                a = fracs[t - 1, pl.ds(p0 + r, PART), :]
                s = offs[t - 1, pl.ds(p0 + r, PART), :]
                if forward:
                    s = -s
                back_one = s < 0.0
                same = s == 0.0
                u1, u2 = u[f, first + 1, part], u[f, first + 2, part]
                h = jnp.where(back_one, u[f, first, part], jnp.where(same, u1, u2))
                for j in range(first, last):
                    u3 = u[f, j + 3, part]
                    h2 = jnp.where(back_one, u1, jnp.where(same, u2, u3))
                    if forward:
                        consume(j, r, h2 + a * (h - h2))
                    else:
                        consume(j, r, h + a * (h2 - h))
                    u1, u2, h = u2, u3, h2

        def sweep_fields(base, sums):
            norm = [sums]
            tasks = []

            def stage(kind, wide, source, rest):
                for f in range(batch):

                    def multiply(f=f):
                        rows = (lz if source is None else source.at[f])[0 : wide * CHUNK, :]
                        product = fold(dot(rows, mats[kind, base + f]))
                        u[f, 0:wide] = product.reshape(wide, CHUNK, LANE)

                    def follow(f=f):
                        rest(f, wide)

                    tasks.append((multiply, follow))

            def row_of(f):
                return hcoef[pl.ds(base + f, 1), :]

            def adjoint(t, force):
                def rest(f, wide):
                    row = row_of(f)

                    def keep(j, r, value):
                        value = value + row * force[j, r : r + PART]
                        split_to(low.at[f], j * CHUNK + r, value)

                    advect(f, t, False, 0, wide - 3, keep)

                return rest

            def leave(t, f, target, wide):
                def keep(j, r, value):
                    split_to(target, j * CHUNK + r, value)

                advect(f, t, True, 0, wide - 3, keep)

            def arrive(f, wide):
                def keep(j, r, value):
                    lon = j + begin
                    if full:
                        u[f, j, r : r + PART] = value
                    if 0 <= lon < BAND:
                        out[base + f, lon, pl.ds(p0 + r, PART), :] = value
                        if full:
                            norm[0] = norm[0] + jnp.sum(
                                (value * value).reshape(PART // 8, 8, LANE), axis=0
                            )

                advect(f, 1, False, 0, wide - 3, keep)
                if full:
                    leave(1, f, low.at[f], wide - 3)

            def forward(t, begins):
                def rest(f, wide):
                    row = row_of(f)
                    for lon in range(BAND):
                        heard[t - 1, lon] = heard[t - 1, lon] + row * u[f, lon - begins]
                    leave(t + 1, f, low.at[f] if t == 1 else third.at[base + f], wide)

                return rest

            stage(1, wide3, None, adjoint(3, z2))
            stage(0, wide3 - 3, low, adjoint(2, z1))
            stage(0, wide3 - 6, low, arrive)
            if full:
                stage(2, wide3 - 12, low, forward(1, begin + 2))
                stage(2, wide3 - 15, low, forward(2, begin + 4))
            if batch == 1:
                for multiply, follow in tasks:
                    multiply()
                    follow()
            else:
                tasks[0][0]()
                for n in range(len(tasks)):
                    if n + 1 < len(tasks):
                        tasks[n + 1][0]()
                    tasks[n][1]()
            return norm[0]

        if full:
            heard[...] = jnp.zeros(heard.shape, F32)
        if batch == fields:
            sums = sweep_fields(0, sums)
        else:
            sums = lax.fori_loop(
                0, fields // batch, lambda n, total: sweep_fields(n * batch, total), sums
            )
        if full:
            total = dot(third[0], mats[3, 0])
            for f in range(1, fields):
                total = total + dot(third[f], mats[3, f])
            total = fold(total)
            for t in (1, 2, 3):
                for lon in range(BAND):
                    if t < 3:
                        value = heard[t - 1, lon]
                    else:
                        value = total[lon * CHUNK : (lon + 1) * CHUNK]
                    high, lo = halves(value)
                    to = pl.ds(((t - 1) * BAND + lon) * LANE + p0, CHUNK)
                    ys[to, 0:LANE] = high
                    ys[to, LANE:] = lo
        return sums

    sums = lax.fori_loop(0, LANE // CHUNK, chunk, jnp.zeros((8, LANE), F32))
    if not full:
        return

    upright = jnp.concatenate(
        [down(place[1][:, n : n + LANE].astype(F32), LANE) for n in range(0, slots, LANE)], axis=0
    )
    away = upright - lax.broadcasted_iota(jnp.int32, (slots, LANE), 1).astype(F32)
    for block in range(STEPS * BAND):
        reads[:, block * LANE : (block + 1) * LANE] = jnp.where(
            away == float(block * LANE), 1.0, 0.0
        ).astype(BF16)
    y = fold(dot(reads[...], ys[...]))
    z = w[...] * y
    z_out[0:slots, :] = z
    curve = jnp.sum((z * y).reshape(slots // 8, 8, LANE), axis=0)
    edge_out[...] = edges_of(place[1], jnp.concatenate(halves(z), axis=1))
    line = lax.broadcasted_iota(jnp.int32, (8, LANE), 0)
    one = jnp.sum(sums, axis=0, keepdims=True)
    two = jnp.sum(curve, axis=0, keepdims=True)
    z_out[slots : slots + 8, :] = jnp.where(line == 0, one, jnp.where(line == 1, two, 0.0))
    z_out[slots + 2 : slots + 4, :] = own[slots : slots + 2, :]


def turn_kernel(source, out):
    for lon in range(BAND):
        out[0, lon] = source[0, lon].T


def combine_kernel(*refs):
    *moments, scale, b, c0, c1, increment, residual, held, sems = refs
    total = moments[0][...]
    for part in moments[1:]:
        total = total + part[...]
    total = jnp.sum(total, axis=1, keepdims=True)
    base = total[2:3]
    m1 = total[3:4] / base
    m2 = total[0:1] / base
    m3 = total[1:2] / base
    eps = scale[0:1, 0:1]
    ap = 1.0 / (eps + m1)
    alpha = eps * ap
    beta = (m2 - m1 * m1) * ap * ap
    u = 1.0 + beta - alpha
    curve = eps * (u * u - 2.0 * u * ap * m1 + ap * ap * m2) + (
        u * u * m1 - 2.0 * u * ap * m2 + ap * ap * m3
    )
    a2p = beta / curve
    a2 = eps * a2p
    inc_b = alpha + a2 * u
    inc_c = -(a2 * ap)
    res_b = 1.0 - alpha - a2 * u
    res_c = a2 * ap - ap - a2p * u
    res_d = a2p * ap
    copies = []
    for f in range(b.shape[0]):
        for lon in range(BAND):
            b_now, c_now = b[f, lon], c0[f, lon]
            to = pl.ds(lon, LANE, stride=BAND)
            held[0, f, to, :] = inc_b * b_now + inc_c * c_now
            held[1, f, to, :] = res_b * b_now + res_c * c_now + res_d * c1[f, lon].T
        for n, target in enumerate((increment, residual)):
            copy = pltpu.make_async_copy(held.at[n, f], target.at[f], sems.at[n, f])
            copy.start()
            copies.append(copy)
    for copy in copies:
        copy.wait()


def params(mebibytes):
    return pltpu.CompilerParams(vmem_limit_bytes=mebibytes * 1024 * 1024)


def shards(
    obs_owner, obs_lonpos, obs_lat, obs_step, obs_top, innovation, obs_weight,
    wind_shift, wind_frac, vmix, hcoef,
):
    devices = lax.axis_size("lon")
    fields = vmix.shape[0]
    count = obs_owner.shape[0]
    cap = max(2, 2 * count // devices)
    slots = devices * cap
    shape = jax.ShapeDtypeStruct
    state = shape((fields, BAND, LANE, LANE), F32)
    rows = shape((slots, LANE), F32)
    edge = shape((2 * LANE, LANE), F32)
    small = shape((8, LANE), F32)
    more_rows = shape((slots + 8, LANE), F32)

    send = pl.pallas_call(
        pack_kernel,
        out_shape=shape((devices, 2 * cap + 8, LANE), F32),
        in_specs=[pl.BlockSpec(memory_space=pltpu.HBM)] * 7,
        scratch_shapes=[pltpu.VMEM((slots, LANE), F32)] * 2
        + [pltpu.VMEM((1, count), jnp.int32)] * 5
        + [pltpu.VMEM((LANE, count), F32)] * 2
        + [pltpu.SemaphoreType.DMA((7,))],
        compiler_params=params(60),
        name="pack",
    )(
        obs_owner.reshape(1, count), obs_lonpos.reshape(1, count), obs_lat.reshape(1, count),
        obs_step.reshape(1, count), obs_top.reshape(1, count), innovation, obs_weight,
    )
    mats, offs, fracs, scale = pl.pallas_call(
        prepare_kernel,
        out_shape=(
            shape((4, fields, 2 * LANE, 2 * LANE), BF16),
            shape((STEPS, LANE, LANE), F32),
            shape((STEPS, LANE, LANE), F32),
            small,
        ),
        compiler_params=params(28),
        name="prepare",
    )(wind_shift, wind_frac, vmix, hcoef)
    received = lax.all_to_all(send, "lon", split_axis=0, concat_axis=0, tiled=True)
    w, rows_d, edge_d = pl.pallas_call(
        unpack_kernel,
        out_shape=(rows, shape((slots + 8, LANE), F32), edge),
        compiler_params=params(28),
        name="unpack",
    )(received, scale)

    def along(value, hop):
        return lax.ppermute(value, "lon", [(i, (i + hop) % devices) for i in range(devices)])

    def swap(value, first):
        pairs = [((i + first) % devices, (i + 1 + first) % devices) for i in range(0, devices, 2)]
        return lax.ppermute(value, "lon", pairs + [(b, a) for a, b in pairs])

    def near(value):
        return swap(value, 0), value, swap(value, 1)

    def far(edges):
        return along(edges[LANE:], 2), along(edges[:LANE], -2)

    def scratch(full, size, batch, begin, end):
        wide = [b - a for a, b in regions(begin, end)]
        shapes = [
            pltpu.VMEM((3, STEPS * BAND * size, slots), BF16),
            pltpu.VMEM((3, LANE, slots), BF16),
            pltpu.VMEM((3, STEPS * BAND, 16, slots), BF16),
            pltpu.VMEM((3, slots, 2 * LANE), BF16),
            pltpu.VMEM((wide[0], size, LANE), F32),
            pltpu.VMEM((wide[1], size, LANE), F32),
            pltpu.VMEM((wide[2] * size, 2 * LANE), BF16),
            pltpu.VMEM((batch, wide[2], size, LANE), F32),
            pltpu.VMEM((batch, wide[1] * size, 2 * LANE), BF16),
        ]
        if full:
            shapes.append(pltpu.VMEM((STEPS * BAND * LANE, 2 * LANE), BF16))
            shapes.append(pltpu.VMEM((slots, STEPS * BAND * LANE), BF16))
            shapes.append(pltpu.VMEM((fields, BAND * size, 2 * LANE), BF16))
            shapes.append(pltpu.VMEM((2, BAND, size, LANE), F32))
        return shapes

    def specs(count):
        return [pl.BlockSpec(memory_space=pltpu.SMEM)] + [
            pl.BlockSpec(memory_space=pltpu.VMEM)
        ] * count

    def cost(columns):
        return pl.CostEstimate(
            flops=columns * fields * LANE * 8 * LANE * LANE,
            bytes_accessed=8 * 1024 * 1024,
            transcendentals=0,
        )

    odd = (lax.axis_index("lon") % 2).reshape(1)

    def sweep(rows_near, edges, facts, size, batch, behind):
        return pl.pallas_call(
            functools.partial(sweep_kernel, True, size, batch, -6, BAND + 3),
            out_shape=(state, more_rows, edge),
            in_specs=specs(13) + [pl.BlockSpec(memory_space=pl.ANY)],
            scratch_shapes=scratch(True, size, batch, -6, BAND + 3),
            compiler_params=params(28),
            cost_estimate=cost(130),
            name="sweep",
        )(odd, *rows_near, *facts, *far(edges), mats, offs, fracs, hcoef, w, behind)

    block = pl.BlockSpec((1, BAND, LANE, LANE), lambda f: (f, 0, 0, 0))

    def turn(value):
        return pl.pallas_call(
            turn_kernel,
            out_shape=state,
            grid=(fields,),
            in_specs=[block],
            out_specs=block,
            compiler_params=params(28),
            cost_estimate=cost(8),
            name="turn",
        )(value)

    facts = near(rows_d)
    b, z0, edge0 = sweep(facts, edge_d, facts, 32, fields, scale)
    b = turn(b)
    c0, z1, _ = sweep(near(z0), edge0, facts, 32, fields, b)
    c0 = turn(c0)
    last = near(z1)
    c1 = pl.pallas_call(
        functools.partial(sweep_kernel, False, 32, fields, 0, BAND),
        out_shape=state,
        in_specs=specs(10) + [pl.BlockSpec(memory_space=pl.ANY)],
        scratch_shapes=scratch(False, 32, fields, 0, BAND),
        compiler_params=params(28),
        cost_estimate=cost(60),
        name="last_sweep",
    )(odd, *last, *facts, mats, offs, fracs, hcoef, c0)

    single = z1[slots:]
    window = last[0][slots:] + single + last[2][slots:]
    covered, parts = 3, [window]
    while devices // covered > 1:
        window = functools.reduce(jnp.add, parts)
        count_of = min(devices // covered, 7)
        parts = [window] + [along(window, -k * covered) for k in range(1, count_of)]
        covered = covered * count_of
    parts = parts + [along(single, -(k - 1)) for k in range(covered, devices)]

    flat = shape((fields, LANE * BAND, LANE), F32)
    increment, residual = pl.pallas_call(
        combine_kernel,
        out_shape=(flat, flat),
        in_specs=[pl.BlockSpec(memory_space=pltpu.VMEM)] * (len(parts) + 4),
        out_specs=[pl.BlockSpec(memory_space=pl.ANY)] * 2,
        scratch_shapes=[
            pltpu.VMEM((2, fields, LANE * BAND, LANE), F32),
            pltpu.SemaphoreType.DMA((2, fields)),
        ],
        compiler_params=params(28),
        cost_estimate=cost(8),
        name="combine",
    )(*parts, scale, b, c0, c1)
    whole = (fields, LANE, BAND, LANE)
    return increment.reshape(whole), residual.reshape(whole)


def solution(mesh):
    profile = P(("member", "lon"))
    field = P("member", None, "lon", None)
    return jax.shard_map(
        shards,
        mesh=mesh,
        in_specs=(P("lon", "member"),) + (profile,) * 4 + (P("member", "lon"),) * 2 + (P(),) * 4,
        out_specs=(field, field),
        check_vma=False,
    )
```

```python
import functools

import jax
import jax.numpy as jnp
from jax import lax
from jax.experimental import pallas as pl
from jax.experimental.pallas import tpu as pltpu
from jax.sharding import PartitionSpec as P

F32 = jnp.float32
BF16 = jnp.bfloat16
BAND = 8
LANE = 128
STEPS = 3
PART = 16

NN = (((1,), (0,)), ((), ()))
NT = (((1,), (1,)), ((), ()))


def dot(left, right, dims=NN):
    return lax.dot_general(left, right, dims, preferred_element_type=F32)


def halves(value):
    high = value.astype(BF16)
    return high, (value - high.astype(F32)).astype(BF16)


def thirds(value):
    high = value.astype(BF16)
    rest = value - high.astype(F32)
    middle = rest.astype(BF16)
    return high, middle, (rest - middle.astype(F32)).astype(BF16)


def fold(product):
    return product[:, :LANE] + product[:, LANE:]


def down(row, count):
    return jnp.broadcast_to(row, (LANE, row.shape[1])).T[:, :count]


def pack_kernel(*refs):
    sources, (out, w_rows, d_rows), held = refs[:7], refs[7:10], refs[10:17]
    copies = [
        pltpu.make_async_copy(source, place, refs[17].at[n])
        for n, (source, place) in enumerate(zip(sources, held))
    ]
    for copy in copies:
        copy.start()
    for copy in copies:
        copy.wait()
    owner, lonpos, lat, step, top, innovation, weight = held
    devices, block, _ = out.shape
    count = owner.shape[1]
    slots = w_rows.shape[0]
    cap = slots // devices
    owners = owner[...].astype(F32)
    upright = down(owners, LANE)
    upright = jnp.concatenate([upright] * (count // LANE), axis=1)
    earlier = lax.broadcasted_iota(jnp.int32, (count, count), 0) < lax.broadcasted_iota(
        jnp.int32, (count, count), 1
    )
    same = jnp.where((upright == owners) & earlier, 1.0, 0.0)
    rank = jnp.sum(same, axis=0, keepdims=True)
    slot = (owners * cap + rank).astype(jnp.int32)
    onehot = jnp.where(
        lax.broadcasted_iota(jnp.int32, (slots, count), 0) == slot, 1.0, 0.0
    ).astype(BF16)
    seen = lax.broadcasted_iota(jnp.int32, (LANE, count), 0) < top[...]
    weights = jnp.where(seen, weight[...], 0.0)
    parts = thirds(weights) + thirds(weights * innovation[...])
    rows = dot(onehot, jnp.concatenate(parts, axis=0), NT)
    w_rows[...] = rows[:, 0:128] + rows[:, 128:256] + rows[:, 256:384]
    d_rows[...] = rows[:, 384:512] + rows[:, 512:640] + rows[:, 640:768]
    line = lax.broadcasted_iota(jnp.int32, (8, count), 0)
    facts = jnp.where(
        line == 0, lonpos[...], jnp.where(line == 1, lat[...], jnp.where(line == 2, step[...], 0))
    )
    facts = dot(facts.astype(F32).astype(BF16), onehot, NT)
    first = lax.broadcasted_iota(jnp.int32, (8, LANE), 0) == 0
    inside = lax.broadcasted_iota(jnp.int32, (8, LANE), 1) < cap
    for dest in range(devices):
        out[dest, 0:cap, :] = w_rows[dest * cap : (dest + 1) * cap, :]
        out[dest, cap : 2 * cap, :] = d_rows[dest * cap : (dest + 1) * cap, :]
        at = dest * cap // LANE * LANE
        tile = facts[:, at : at + LANE]
        if dest * cap != at:
            tile = pltpu.roll(tile, LANE - (dest * cap - at), 1)
        column = tile[0:1] * float(LANE) + tile[1:2]
        tile = jnp.where(first, column, tile[2:3])
        out[dest, 2 * cap : 2 * cap + 8, :] = jnp.where(inside, tile, 0.0)


def prepare_kernel(shift, frac, vmix, hcoef, mats, offs, fracs, scale):
    fields = vmix.shape[0]
    for t in range(STEPS):
        offs[t] = shift[t].astype(F32).T
        fracs[t] = frac[t].T
    bound = jnp.zeros((1, 1), F32)
    reach = jnp.zeros((1, LANE), F32)
    for f in range(fields):
        v = vmix[f]
        size = jnp.abs(v)
        over = jnp.max(jnp.sum(size, axis=0, keepdims=True), axis=1, keepdims=True)
        along = jnp.max(jnp.sum(size, axis=1, keepdims=True), axis=0, keepdims=True)
        bound = jnp.maximum(bound, over * along)
        row = hcoef[f : f + 1, :]
        reach = reach + row * row
        turned = v.T
        weighed = turned * row
        for kind, matrix in enumerate((v, weighed.T, turned, weighed)):
            high, low = halves(matrix)
            both = jnp.concatenate([high, low], axis=1)
            mats[kind, f] = jnp.concatenate([both, both], axis=0)
    rho = bound * bound * bound * jnp.max(reach, axis=1, keepdims=True) * 2.0
    rho = jnp.minimum(jnp.maximum(rho, 1e-18), 1e18)
    scale[...] = jnp.broadcast_to(1.0 / rho, (8, LANE))


def place_of(column, step):
    return (step - 1.0) * float(BAND * LANE) + column


def line_of(ref, first, count):
    return jnp.concatenate([ref[first + n : first + n + 1, :] for n in range(count)], axis=1)


def places(ref, slots):
    groups = slots // LANE
    return place_of(line_of(ref, slots, groups), line_of(ref, slots + groups, groups)).astype(
        jnp.int32
    )


def lat_onehot(place, first, count):
    rows = lax.broadcasted_iota(jnp.int32, (count, place.shape[1]), 0) + first
    return jnp.where((place & (LANE - 1)) == rows, 1.0, 0.0).astype(BF16)


def block_mask(place, block, count):
    wide = jnp.broadcast_to(place >> 7, (count, place.shape[1]))
    return jnp.where(wide == block, 1.0, 0.0).astype(BF16)


def edges_of(place, both):
    lats = lat_onehot(place, 0, LANE)
    first = lats * block_mask(place, (STEPS - 1) * BAND, LANE)
    last = lats * block_mask(place, STEPS * BAND - 1, LANE)
    return fold(dot(jnp.concatenate([first, last], axis=0), both))


def unpack_kernel(received, scale, w_out, ex_out, edge_out):
    devices = received.shape[0]
    slots = w_out.shape[0]
    cap = slots // devices
    per = LANE // cap
    groups = slots // LANE
    shrink = scale[0:1, :]
    lines = [jnp.zeros((8, LANE), F32) for _ in range(groups)]
    for source in range(devices):
        at = source * cap
        w_out[at : at + cap, :] = received[source, 0:cap, :] * shrink
        ex_out[at : at + cap, :] = received[source, cap : 2 * cap, :]
        tile = received[source, 2 * cap : 2 * cap + 8, :]
        if source % per:
            tile = pltpu.roll(tile, cap * (source % per), 1)
        lines[source // per] = lines[source // per] + tile
    for n in range(groups):
        ex_out[slots + n : slots + n + 1, :] = lines[n][0:1]
        ex_out[slots + groups + n : slots + groups + n + 1, :] = lines[n][1:2]
    place = places(ex_out, slots)
    both = jnp.concatenate(halves(ex_out[0:slots, :]), axis=1)
    edge_out[...] = edges_of(place, both)


def regions(begin, end):
    return [(begin - t, end + 2 * t) for t in range(1, STEPS + 1)]


def sweep_kernel(full, chunk_size, batch, begin, end, *refs):
    CHUNK = chunk_size
    if full:
        (odd, inner, own, outer, m_inner, m_own, m_outer, e_left, e_right, mats, offs, fracs,
         hcoef, w, _, out, z_out, edge_out, *scratch) = refs
        sel, lats, masks, zs, z1, z2, lz, u, low, ys, reads, third, heard = scratch
    else:
        (odd, inner, own, outer, m_inner, m_own, m_outer, mats, offs, fracs, hcoef, _,
         out, *scratch) = refs
        sel, lats, masks, zs, z1, z2, lz, u, low = scratch
    fields = mats.shape[1]
    slots = zs.shape[1]
    spans = regions(begin, end)
    swapped = odd[0]

    def choose(one, other):
        return jnp.where(jnp.broadcast_to(swapped, one.shape) == 1, one, other)

    near = (inner[0:slots, :], outer[0:slots, :])
    rows_of = (choose(near[0], near[1]), own[0:slots, :], choose(near[1], near[0]))
    near = (places(m_inner, slots), places(m_outer, slots))
    place = (choose(near[0], near[1]), places(m_own, slots), choose(near[1], near[0]))
    blocks = []
    for band in range(3):
        shift = (band - 1) * BAND
        blocks.append(
            [
                (t, i, i + shift - spans[t - 1][0])
                for t in range(1, STEPS + 1)
                for i in range(BAND)
                if spans[t - 1][0] <= i + shift < spans[t - 1][1]
            ]
        )
        high, lo = halves(rows_of[band])
        zs[band, :, 0:LANE] = high
        zs[band, :, LANE:] = lo
        lats[band] = lat_onehot(place[band], 0, LANE)
        for t, i, _ in blocks[band]:
            masks[band, (t - 1) * BAND + i] = block_mask(place[band], (t - 1) * BAND + i, 16)

    wide3 = spans[2][1] - spans[2][0]

    def split_to(ref, at, value):
        high, lo = halves(value)
        ref[at : at + value.shape[0], 0:LANE] = high
        ref[at : at + value.shape[0], LANE:] = lo

    def chunk(c, sums):
        p0 = pl.multiple_of(c * CHUNK, CHUNK)
        here = pl.ds(p0, CHUNK)
        for band in range(3):
            count = len(blocks[band])
            for n, (t, i, _) in enumerate(blocks[band]):
                mask = masks[band, (t - 1) * BAND + i]
                mask = jnp.concatenate([mask] * (CHUNK // 16), axis=0)
                sel[band, n * CHUNK : (n + 1) * CHUNK, :] = lats[band, here, :] * mask
            dense = fold(dot(sel[band, 0 : count * CHUNK, :], zs[band]))
            for n, (t, i, at) in enumerate(blocks[band]):
                slab = dense[n * CHUNK : (n + 1) * CHUNK]
                if t == 3:
                    split_to(lz, at * CHUNK, slab)
                else:
                    (z1 if t == 1 else z2)[at] = slab
        if full:
            split_to(lz, 0, e_left[here, :])
            split_to(lz, (wide3 - 1) * CHUNK, e_right[here, :])

        def advect(f, t, forward, first, last, consume):
            for r in range(0, CHUNK, PART):
                part = slice(r, r + PART)
                a = fracs[t - 1, pl.ds(p0 + r, PART), :]
                s = offs[t - 1, pl.ds(p0 + r, PART), :]
                if forward:
                    s = -s
                back_one = s < 0.0
                same = s == 0.0
                u1, u2 = u[f, first + 1, part], u[f, first + 2, part]
                h = jnp.where(back_one, u[f, first, part], jnp.where(same, u1, u2))
                for j in range(first, last):
                    u3 = u[f, j + 3, part]
                    h2 = jnp.where(back_one, u1, jnp.where(same, u2, u3))
                    if forward:
                        consume(j, r, h2 + a * (h - h2))
                    else:
                        consume(j, r, h + a * (h2 - h))
                    u1, u2, h = u2, u3, h2

        def sweep_fields(base, sums):
            norm = [sums]
            tasks = []

            def stage(kind, wide, source, rest):
                for f in range(batch):

                    def multiply(f=f):
                        rows = (lz if source is None else source.at[f])[0 : wide * CHUNK, :]
                        product = fold(dot(rows, mats[kind, base + f]))
                        u[f, 0:wide] = product.reshape(wide, CHUNK, LANE)

                    def follow(f=f):
                        rest(f, wide)

                    tasks.append((multiply, follow))

            def row_of(f):
                return hcoef[pl.ds(base + f, 1), :]

            def adjoint(t, force):
                def rest(f, wide):
                    row = row_of(f)

                    def keep(j, r, value):
                        value = value + row * force[j, r : r + PART]
                        split_to(low.at[f], j * CHUNK + r, value)

                    advect(f, t, False, 0, wide - 3, keep)

                return rest

            def leave(t, f, target, wide):
                def keep(j, r, value):
                    split_to(target, j * CHUNK + r, value)

                advect(f, t, True, 0, wide - 3, keep)

            def arrive(f, wide):
                def keep(j, r, value):
                    lon = j + begin
                    if full:
                        u[f, j, r : r + PART] = value
                    if 0 <= lon < BAND:
                        out[base + f, lon, pl.ds(p0 + r, PART), :] = value
                        if full:
                            norm[0] = norm[0] + jnp.sum(
                                (value * value).reshape(PART // 8, 8, LANE), axis=0
                            )

                advect(f, 1, False, 0, wide - 3, keep)
                if full:
                    leave(1, f, low.at[f], wide - 3)

            def forward(t, begins):
                def rest(f, wide):
                    row = row_of(f)
                    for lon in range(BAND):
                        heard[t - 1, lon] = heard[t - 1, lon] + row * u[f, lon - begins]
                    leave(t + 1, f, low.at[f] if t == 1 else third.at[base + f], wide)

                return rest

            stage(1, wide3, None, adjoint(3, z2))
            stage(0, wide3 - 3, low, adjoint(2, z1))
            stage(0, wide3 - 6, low, arrive)
            if full:
                stage(2, wide3 - 12, low, forward(1, begin + 2))
                stage(2, wide3 - 15, low, forward(2, begin + 4))
            if batch == 1:
                for multiply, follow in tasks:
                    multiply()
                    follow()
            else:
                tasks[0][0]()
                for n in range(len(tasks)):
                    if n + 1 < len(tasks):
                        tasks[n + 1][0]()
                    tasks[n][1]()
            return norm[0]

        if full:
            heard[...] = jnp.zeros(heard.shape, F32)
        if batch == fields:
            sums = sweep_fields(0, sums)
        else:
            sums = lax.fori_loop(
                0, fields // batch, lambda n, total: sweep_fields(n * batch, total), sums
            )
        if full:
            total = dot(third[0], mats[3, 0])
            for f in range(1, fields):
                total = total + dot(third[f], mats[3, f])
            total = fold(total)
            for t in (1, 2, 3):
                for lon in range(BAND):
                    if t < 3:
                        value = heard[t - 1, lon]
                    else:
                        value = total[lon * CHUNK : (lon + 1) * CHUNK]
                    high, lo = halves(value)
                    to = pl.ds(((t - 1) * BAND + lon) * LANE + p0, CHUNK)
                    ys[to, 0:LANE] = high
                    ys[to, LANE:] = lo
        return sums

    sums = lax.fori_loop(0, LANE // CHUNK, chunk, jnp.zeros((8, LANE), F32))
    if not full:
        return

    upright = jnp.concatenate(
        [down(place[1][:, n : n + LANE].astype(F32), LANE) for n in range(0, slots, LANE)], axis=0
    )
    away = upright - lax.broadcasted_iota(jnp.int32, (slots, LANE), 1).astype(F32)
    for block in range(STEPS * BAND):
        reads[:, block * LANE : (block + 1) * LANE] = jnp.where(
            away == float(block * LANE), 1.0, 0.0
        ).astype(BF16)
    y = fold(dot(reads[...], ys[...]))
    z = w[...] * y
    z_out[0:slots, :] = z
    curve = jnp.sum((z * y).reshape(slots // 8, 8, LANE), axis=0)
    edge_out[...] = edges_of(place[1], jnp.concatenate(halves(z), axis=1))
    line = lax.broadcasted_iota(jnp.int32, (8, LANE), 0)
    one = jnp.sum(sums, axis=0, keepdims=True)
    two = jnp.sum(curve, axis=0, keepdims=True)
    z_out[slots : slots + 8, :] = jnp.where(line == 0, one, jnp.where(line == 1, two, 0.0))
    z_out[slots + 2 : slots + 4, :] = own[slots : slots + 2, :]


def turn_kernel(source, out):
    for lon in range(BAND):
        out[0, lon] = source[0, lon].T


def combine_kernel(*refs):
    *moments, scale, b, c0, c1, increment, residual, held, sems = refs
    total = moments[0][...]
    for part in moments[1:]:
        total = total + part[...]
    total = jnp.sum(total, axis=1, keepdims=True)
    base = total[2:3]
    m1 = total[3:4] / base
    m2 = total[0:1] / base
    m3 = total[1:2] / base
    eps = scale[0:1, 0:1]
    ap = 1.0 / (eps + m1)
    alpha = eps * ap
    beta = (m2 - m1 * m1) * ap * ap
    u = 1.0 + beta - alpha
    curve = eps * (u * u - 2.0 * u * ap * m1 + ap * ap * m2) + (
        u * u * m1 - 2.0 * u * ap * m2 + ap * ap * m3
    )
    a2p = beta / curve
    a2 = eps * a2p
    inc_b = alpha + a2 * u
    inc_c = -(a2 * ap)
    res_b = 1.0 - alpha - a2 * u
    res_c = a2 * ap - ap - a2p * u
    res_d = a2p * ap
    copies = []
    for f in range(b.shape[0]):
        for lon in range(BAND):
            b_now, c_now = b[f, lon], c0[f, lon]
            to = pl.ds(lon, LANE, stride=BAND)
            held[0, f, to, :] = inc_b * b_now + inc_c * c_now
            held[1, f, to, :] = res_b * b_now + res_c * c_now + res_d * c1[f, lon].T
        for n, target in enumerate((increment, residual)):
            copy = pltpu.make_async_copy(held.at[n, f], target.at[f], sems.at[n, f])
            copy.start()
            copies.append(copy)
    for copy in copies:
        copy.wait()


def params(mebibytes):
    return pltpu.CompilerParams(vmem_limit_bytes=mebibytes * 1024 * 1024)


def shards(
    obs_owner, obs_lonpos, obs_lat, obs_step, obs_top, innovation, obs_weight,
    wind_shift, wind_frac, vmix, hcoef,
):
    devices = lax.axis_size("lon")
    fields = vmix.shape[0]
    count = obs_owner.shape[0]
    cap = max(2, 2 * count // devices)
    slots = devices * cap
    shape = jax.ShapeDtypeStruct
    state = shape((fields, BAND, LANE, LANE), F32)
    rows = shape((slots, LANE), F32)
    edge = shape((2 * LANE, LANE), F32)
    small = shape((8, LANE), F32)
    more_rows = shape((slots + 8, LANE), F32)

    send = pl.pallas_call(
        pack_kernel,
        out_shape=shape((devices, 2 * cap + 8, LANE), F32),
        in_specs=[pl.BlockSpec(memory_space=pltpu.HBM)] * 7,
        scratch_shapes=[pltpu.VMEM((slots, LANE), F32)] * 2
        + [pltpu.VMEM((1, count), jnp.int32)] * 5
        + [pltpu.VMEM((LANE, count), F32)] * 2
        + [pltpu.SemaphoreType.DMA((7,))],
        compiler_params=params(60),
        name="pack",
    )(
        obs_owner.reshape(1, count), obs_lonpos.reshape(1, count), obs_lat.reshape(1, count),
        obs_step.reshape(1, count), obs_top.reshape(1, count), innovation, obs_weight,
    )
    mats, offs, fracs, scale = pl.pallas_call(
        prepare_kernel,
        out_shape=(
            shape((4, fields, 2 * LANE, 2 * LANE), BF16),
            shape((STEPS, LANE, LANE), F32),
            shape((STEPS, LANE, LANE), F32),
            small,
        ),
        compiler_params=params(44),
        name="prepare",
    )(wind_shift, wind_frac, vmix, hcoef)
    received = lax.all_to_all(send, "lon", split_axis=0, concat_axis=0, tiled=True)
    w, rows_d, edge_d = pl.pallas_call(
        unpack_kernel,
        out_shape=(rows, shape((slots + 8, LANE), F32), edge),
        compiler_params=params(44),
        name="unpack",
    )(received, scale)

    def along(value, hop):
        return lax.ppermute(value, "lon", [(i, (i + hop) % devices) for i in range(devices)])

    def swap(value, first):
        pairs = [((i + first) % devices, (i + 1 + first) % devices) for i in range(0, devices, 2)]
        return lax.ppermute(value, "lon", pairs + [(b, a) for a, b in pairs])

    def near(value):
        return swap(value, 0), value, swap(value, 1)

    def far(edges):
        return along(edges[LANE:], 2), along(edges[:LANE], -2)

    def scratch(full, size, batch, begin, end):
        wide = [b - a for a, b in regions(begin, end)]
        shapes = [
            pltpu.VMEM((3, STEPS * BAND * size, slots), BF16),
            pltpu.VMEM((3, LANE, slots), BF16),
            pltpu.VMEM((3, STEPS * BAND, 16, slots), BF16),
            pltpu.VMEM((3, slots, 2 * LANE), BF16),
            pltpu.VMEM((wide[0], size, LANE), F32),
            pltpu.VMEM((wide[1], size, LANE), F32),
            pltpu.VMEM((wide[2] * size, 2 * LANE), BF16),
            pltpu.VMEM((batch, wide[2], size, LANE), F32),
            pltpu.VMEM((batch, wide[1] * size, 2 * LANE), BF16),
        ]
        if full:
            shapes.append(pltpu.VMEM((STEPS * BAND * LANE, 2 * LANE), BF16))
            shapes.append(pltpu.VMEM((slots, STEPS * BAND * LANE), BF16))
            shapes.append(pltpu.VMEM((fields, BAND * size, 2 * LANE), BF16))
            shapes.append(pltpu.VMEM((2, BAND, size, LANE), F32))
        return shapes

    def specs(count):
        return [pl.BlockSpec(memory_space=pltpu.SMEM)] + [
            pl.BlockSpec(memory_space=pltpu.VMEM)
        ] * count

    def cost(columns):
        return pl.CostEstimate(
            flops=columns * fields * LANE * 8 * LANE * LANE,
            bytes_accessed=8 * 1024 * 1024,
            transcendentals=0,
        )

    odd = (lax.axis_index("lon") % 2).reshape(1)

    def sweep(rows_near, edges, facts, size, batch, behind):
        return pl.pallas_call(
            functools.partial(sweep_kernel, True, size, batch, -6, BAND + 3),
            out_shape=(state, more_rows, edge),
            in_specs=specs(13) + [pl.BlockSpec(memory_space=pl.ANY)],
            scratch_shapes=scratch(True, size, batch, -6, BAND + 3),
            compiler_params=params(44),
            cost_estimate=cost(130),
            name="sweep",
        )(odd, *rows_near, *facts, *far(edges), mats, offs, fracs, hcoef, w, behind)

    block = pl.BlockSpec((1, BAND, LANE, LANE), lambda f: (f, 0, 0, 0))

    def turn(value):
        return pl.pallas_call(
            turn_kernel,
            out_shape=state,
            grid=(fields,),
            in_specs=[block],
            out_specs=block,
            compiler_params=params(44),
            cost_estimate=cost(8),
            name="turn",
        )(value)

    facts = near(rows_d)
    b, z0, edge0 = sweep(facts, edge_d, facts, 32, fields, scale)
    b = turn(b)
    c0, z1, _ = sweep(near(z0), edge0, facts, 32, fields, b)
    c0 = turn(c0)
    last = near(z1)
    c1 = pl.pallas_call(
        functools.partial(sweep_kernel, False, 32, fields, 0, BAND),
        out_shape=state,
        in_specs=specs(10) + [pl.BlockSpec(memory_space=pl.ANY)],
        scratch_shapes=scratch(False, 32, fields, 0, BAND),
        compiler_params=params(44),
        cost_estimate=cost(60),
        name="last_sweep",
    )(odd, *last, *facts, mats, offs, fracs, hcoef, c0)

    single = z1[slots:]
    window = last[0][slots:] + single + last[2][slots:]
    covered, parts = 3, [window]
    while devices // covered > 1:
        window = functools.reduce(jnp.add, parts)
        count_of = min(devices // covered, 7)
        parts = [window] + [along(window, -k * covered) for k in range(1, count_of)]
        covered = covered * count_of
    parts = parts + [along(single, -(k - 1)) for k in range(covered, devices)]

    flat = shape((fields, LANE * BAND, LANE), F32)
    increment, residual = pl.pallas_call(
        combine_kernel,
        out_shape=(flat, flat),
        in_specs=[pl.BlockSpec(memory_space=pltpu.VMEM)] * (len(parts) + 4),
        out_specs=[pl.BlockSpec(memory_space=pl.ANY)] * 2,
        scratch_shapes=[
            pltpu.VMEM((2, fields, LANE * BAND, LANE), F32),
            pltpu.SemaphoreType.DMA((2, fields)),
        ],
        compiler_params=params(44),
        cost_estimate=cost(8),
        name="combine",
    )(*parts, scale, b, c0, c1)
    whole = (fields, LANE, BAND, LANE)
    return increment.reshape(whole), residual.reshape(whole)


def solution(mesh):
    profile = P(("member", "lon"))
    field = P("member", None, "lon", None)
    return jax.shard_map(
        shards,
        mesh=mesh,
        in_specs=(P("lon", "member"),) + (profile,) * 4 + (P("member", "lon"),) * 2 + (P(),) * 4,
        out_specs=(field, field),
        check_vma=False,
    )
```

```python
import functools

import jax
import jax.numpy as jnp
from jax import lax
from jax.experimental import pallas as pl
from jax.experimental.pallas import tpu as pltpu
from jax.sharding import PartitionSpec as P

F32 = jnp.float32
BF16 = jnp.bfloat16
BAND = 8
LANE = 128
STEPS = 3
PART = 16

NN = (((1,), (0,)), ((), ()))
NT = (((1,), (1,)), ((), ()))


def dot(left, right, dims=NN):
    return lax.dot_general(left, right, dims, preferred_element_type=F32)


def halves(value):
    high = value.astype(BF16)
    return high, (value - high.astype(F32)).astype(BF16)


def thirds(value):
    high = value.astype(BF16)
    rest = value - high.astype(F32)
    middle = rest.astype(BF16)
    return high, middle, (rest - middle.astype(F32)).astype(BF16)


def fold(product):
    return product[:, :LANE] + product[:, LANE:]


def down(row, count):
    return jnp.broadcast_to(row, (LANE, row.shape[1])).T[:, :count]


def pack_kernel(*refs):
    sources, (out, w_rows, d_rows), held = refs[:7], refs[7:10], refs[10:17]
    copies = [
        pltpu.make_async_copy(source, place, refs[17].at[n])
        for n, (source, place) in enumerate(zip(sources, held))
    ]
    for copy in copies:
        copy.start()
    for copy in copies:
        copy.wait()
    owner, lonpos, lat, step, top, innovation, weight = held
    devices, block, _ = out.shape
    count = owner.shape[1]
    slots = w_rows.shape[0]
    cap = slots // devices
    owners = owner[...].astype(F32)
    upright = down(owners, LANE)
    upright = jnp.concatenate([upright] * (count // LANE), axis=1)
    earlier = lax.broadcasted_iota(jnp.int32, (count, count), 0) < lax.broadcasted_iota(
        jnp.int32, (count, count), 1
    )
    same = jnp.where((upright == owners) & earlier, 1.0, 0.0)
    rank = jnp.sum(same, axis=0, keepdims=True)
    slot = (owners * cap + rank).astype(jnp.int32)
    onehot = jnp.where(
        lax.broadcasted_iota(jnp.int32, (slots, count), 0) == slot, 1.0, 0.0
    ).astype(BF16)
    seen = lax.broadcasted_iota(jnp.int32, (LANE, count), 0) < top[...]
    weights = jnp.where(seen, weight[...], 0.0)
    parts = thirds(weights) + thirds(weights * innovation[...])
    rows = dot(onehot, jnp.concatenate(parts, axis=0), NT)
    w_rows[...] = rows[:, 0:128] + rows[:, 128:256] + rows[:, 256:384]
    d_rows[...] = rows[:, 384:512] + rows[:, 512:640] + rows[:, 640:768]
    line = lax.broadcasted_iota(jnp.int32, (8, count), 0)
    facts = jnp.where(
        line == 0, lonpos[...], jnp.where(line == 1, lat[...], jnp.where(line == 2, step[...], 0))
    )
    facts = dot(facts.astype(F32).astype(BF16), onehot, NT)
    first = lax.broadcasted_iota(jnp.int32, (8, LANE), 0) == 0
    inside = lax.broadcasted_iota(jnp.int32, (8, LANE), 1) < cap
    for dest in range(devices):
        out[dest, 0:cap, :] = w_rows[dest * cap : (dest + 1) * cap, :]
        out[dest, cap : 2 * cap, :] = d_rows[dest * cap : (dest + 1) * cap, :]
        at = dest * cap // LANE * LANE
        tile = facts[:, at : at + LANE]
        if dest * cap != at:
            tile = pltpu.roll(tile, LANE - (dest * cap - at), 1)
        column = tile[0:1] * float(LANE) + tile[1:2]
        tile = jnp.where(first, column, tile[2:3])
        out[dest, 2 * cap : 2 * cap + 8, :] = jnp.where(inside, tile, 0.0)


def prepare_kernel(shift, frac, vmix, hcoef, mats, offs, fracs, scale):
    fields = vmix.shape[0]
    for t in range(STEPS):
        offs[t] = shift[t].astype(F32).T
        fracs[t] = frac[t].T
    bound = jnp.zeros((1, 1), F32)
    reach = jnp.zeros((1, LANE), F32)
    for f in range(fields):
        v = vmix[f]
        size = jnp.abs(v)
        over = jnp.max(jnp.sum(size, axis=0, keepdims=True), axis=1, keepdims=True)
        along = jnp.max(jnp.sum(size, axis=1, keepdims=True), axis=0, keepdims=True)
        bound = jnp.maximum(bound, over * along)
        row = hcoef[f : f + 1, :]
        reach = reach + row * row
        turned = v.T
        weighed = turned * row
        for kind, matrix in enumerate((v, weighed.T, turned, weighed)):
            high, low = halves(matrix)
            both = jnp.concatenate([high, low], axis=1)
            mats[kind, f] = jnp.concatenate([both, both], axis=0)
    rho = bound * bound * bound * jnp.max(reach, axis=1, keepdims=True) * 2.0
    rho = jnp.minimum(jnp.maximum(rho, 1e-18), 1e18)
    scale[...] = jnp.broadcast_to(1.0 / rho, (8, LANE))


def place_of(column, step):
    return (step - 1.0) * float(BAND * LANE) + column


def line_of(ref, first, count):
    return jnp.concatenate([ref[first + n : first + n + 1, :] for n in range(count)], axis=1)


def places(ref, slots):
    groups = slots // LANE
    return place_of(line_of(ref, slots, groups), line_of(ref, slots + groups, groups)).astype(
        jnp.int32
    )


def lat_onehot(place, first, count):
    rows = lax.broadcasted_iota(jnp.int32, (count, place.shape[1]), 0) + first
    return jnp.where((place & (LANE - 1)) == rows, 1.0, 0.0).astype(BF16)


def block_mask(place, block, count):
    wide = jnp.broadcast_to(place >> 7, (count, place.shape[1]))
    return jnp.where(wide == block, 1.0, 0.0).astype(BF16)


def edges_of(place, both):
    lats = lat_onehot(place, 0, LANE)
    first = lats * block_mask(place, (STEPS - 1) * BAND, LANE)
    last = lats * block_mask(place, STEPS * BAND - 1, LANE)
    return fold(dot(jnp.concatenate([first, last], axis=0), both))


def unpack_kernel(received, scale, w_out, ex_out, edge_out):
    devices = received.shape[0]
    slots = w_out.shape[0]
    cap = slots // devices
    per = LANE // cap
    groups = slots // LANE
    shrink = scale[0:1, :]
    lines = [jnp.zeros((8, LANE), F32) for _ in range(groups)]
    for source in range(devices):
        at = source * cap
        w_out[at : at + cap, :] = received[source, 0:cap, :] * shrink
        ex_out[at : at + cap, :] = received[source, cap : 2 * cap, :]
        tile = received[source, 2 * cap : 2 * cap + 8, :]
        if source % per:
            tile = pltpu.roll(tile, cap * (source % per), 1)
        lines[source // per] = lines[source // per] + tile
    for n in range(groups):
        ex_out[slots + n : slots + n + 1, :] = lines[n][0:1]
        ex_out[slots + groups + n : slots + groups + n + 1, :] = lines[n][1:2]
    place = places(ex_out, slots)
    both = jnp.concatenate(halves(ex_out[0:slots, :]), axis=1)
    edge_out[...] = edges_of(place, both)


def regions(begin, end):
    return [(begin - t, end + 2 * t) for t in range(1, STEPS + 1)]


def sweep_kernel(full, chunk_size, batch, begin, end, *refs):
    CHUNK = chunk_size
    if full:
        (odd, inner, own, outer, m_inner, m_own, m_outer, e_left, e_right, mats, offs, fracs_in,
         hcoef, w_in, _, out, z_out, edge_out, *scratch) = refs
        sel, lats, masks, zs, z1, z2, lz, u, low, fracs, sems, *scratch = scratch
        ys, reads, third, heard, w = scratch
        fetch_w = pltpu.make_async_copy(w_in, w, sems.at[1])
        fetch_w.start()
    else:
        (odd, inner, own, outer, m_inner, m_own, m_outer, mats, offs, fracs_in, hcoef, _,
         out, *scratch) = refs
        sel, lats, masks, zs, z1, z2, lz, u, low, fracs, sems = scratch
    fetch_fracs = pltpu.make_async_copy(fracs_in, fracs, sems.at[0])
    fetch_fracs.start()
    fields = mats.shape[1]
    slots = zs.shape[1]
    spans = regions(begin, end)
    swapped = odd[0]

    def choose(one, other):
        return jnp.where(jnp.broadcast_to(swapped, one.shape) == 1, one, other)

    near = (inner[0:slots, :], outer[0:slots, :])
    rows_of = (choose(near[0], near[1]), own[0:slots, :], choose(near[1], near[0]))
    near = (places(m_inner, slots), places(m_outer, slots))
    place = (choose(near[0], near[1]), places(m_own, slots), choose(near[1], near[0]))
    blocks = []
    for band in range(3):
        shift = (band - 1) * BAND
        blocks.append(
            [
                (t, i, i + shift - spans[t - 1][0])
                for t in range(1, STEPS + 1)
                for i in range(BAND)
                if spans[t - 1][0] <= i + shift < spans[t - 1][1]
            ]
        )
        high, lo = halves(rows_of[band])
        zs[band, :, 0:LANE] = high
        zs[band, :, LANE:] = lo
        lats[band] = lat_onehot(place[band], 0, LANE)
        for t, i, _ in blocks[band]:
            masks[band, (t - 1) * BAND + i] = block_mask(place[band], (t - 1) * BAND + i, 16)

    wide3 = spans[2][1] - spans[2][0]

    def split_to(ref, at, value):
        high, lo = halves(value)
        ref[at : at + value.shape[0], 0:LANE] = high
        ref[at : at + value.shape[0], LANE:] = lo

    def chunk(c, sums):
        p0 = pl.multiple_of(c * CHUNK, CHUNK)
        here = pl.ds(p0, CHUNK)
        for band in range(3):
            count = len(blocks[band])
            for n, (t, i, _) in enumerate(blocks[band]):
                mask = masks[band, (t - 1) * BAND + i]
                mask = jnp.concatenate([mask] * (CHUNK // 16), axis=0)
                sel[band, n * CHUNK : (n + 1) * CHUNK, :] = lats[band, here, :] * mask
            dense = fold(dot(sel[band, 0 : count * CHUNK, :], zs[band]))
            for n, (t, i, at) in enumerate(blocks[band]):
                slab = dense[n * CHUNK : (n + 1) * CHUNK]
                if t == 3:
                    split_to(lz, at * CHUNK, slab)
                else:
                    (z1 if t == 1 else z2)[at] = slab
        if full:
            split_to(lz, 0, e_left[here, :])
            split_to(lz, (wide3 - 1) * CHUNK, e_right[here, :])

        def advect(f, t, forward, first, last, consume):
            for r in range(0, CHUNK, PART):
                part = slice(r, r + PART)
                a = fracs[t - 1, pl.ds(p0 + r, PART), :]
                s = offs[t - 1, pl.ds(p0 + r, PART), :]
                if forward:
                    s = -s
                back_one = s < 0.0
                same = s == 0.0
                u1, u2 = u[f, first + 1, part], u[f, first + 2, part]
                h = jnp.where(back_one, u[f, first, part], jnp.where(same, u1, u2))
                for j in range(first, last):
                    u3 = u[f, j + 3, part]
                    h2 = jnp.where(back_one, u1, jnp.where(same, u2, u3))
                    if forward:
                        consume(j, r, h2 + a * (h - h2))
                    else:
                        consume(j, r, h + a * (h2 - h))
                    u1, u2, h = u2, u3, h2

        def sweep_fields(base, sums):
            norm = [sums]
            tasks = []

            def stage(kind, wide, source, rest):
                for f in range(batch):

                    def multiply(f=f):
                        rows = (lz if source is None else source.at[f])[0 : wide * CHUNK, :]
                        product = fold(dot(rows, mats[kind, base + f]))
                        u[f, 0:wide] = product.reshape(wide, CHUNK, LANE)

                    def follow(f=f):
                        rest(f, wide)

                    tasks.append((multiply, follow))

            def row_of(f):
                return hcoef[pl.ds(base + f, 1), :]

            def adjoint(t, force):
                def rest(f, wide):
                    row = row_of(f)

                    def keep(j, r, value):
                        value = value + row * force[j, r : r + PART]
                        split_to(low.at[f], j * CHUNK + r, value)

                    advect(f, t, False, 0, wide - 3, keep)

                return rest

            def leave(t, f, target, wide):
                def keep(j, r, value):
                    split_to(target, j * CHUNK + r, value)

                advect(f, t, True, 0, wide - 3, keep)

            def arrive(f, wide):
                def keep(j, r, value):
                    lon = j + begin
                    if full:
                        u[f, j, r : r + PART] = value
                    if 0 <= lon < BAND:
                        out[base + f, lon, pl.ds(p0 + r, PART), :] = value
                        if full:
                            norm[0] = norm[0] + jnp.sum(
                                (value * value).reshape(PART // 8, 8, LANE), axis=0
                            )

                advect(f, 1, False, 0, wide - 3, keep)
                if full:
                    leave(1, f, low.at[f], wide - 3)

            def forward(t, begins):
                def rest(f, wide):
                    row = row_of(f)
                    for lon in range(BAND):
                        heard[t - 1, lon] = heard[t - 1, lon] + row * u[f, lon - begins]
                    leave(t + 1, f, low.at[f] if t == 1 else third.at[base + f], wide)

                return rest

            stage(1, wide3, None, adjoint(3, z2))
            stage(0, wide3 - 3, low, adjoint(2, z1))
            stage(0, wide3 - 6, low, arrive)
            if full:
                stage(2, wide3 - 12, low, forward(1, begin + 2))
                stage(2, wide3 - 15, low, forward(2, begin + 4))
            if batch == 1:
                for multiply, follow in tasks:
                    multiply()
                    follow()
            else:
                tasks[0][0]()
                for n in range(len(tasks)):
                    if n + 1 < len(tasks):
                        tasks[n + 1][0]()
                    tasks[n][1]()
            return norm[0]

        if full:
            heard[...] = jnp.zeros(heard.shape, F32)
        if batch == fields:
            sums = sweep_fields(0, sums)
        else:
            sums = lax.fori_loop(
                0, fields // batch, lambda n, total: sweep_fields(n * batch, total), sums
            )
        if full:
            total = dot(third[0], mats[3, 0])
            for f in range(1, fields):
                total = total + dot(third[f], mats[3, f])
            total = fold(total)
            for t in (1, 2, 3):
                for lon in range(BAND):
                    if t < 3:
                        value = heard[t - 1, lon]
                    else:
                        value = total[lon * CHUNK : (lon + 1) * CHUNK]
                    high, lo = halves(value)
                    to = pl.ds(((t - 1) * BAND + lon) * LANE + p0, CHUNK)
                    ys[to, 0:LANE] = high
                    ys[to, LANE:] = lo
        return sums

    fetch_fracs.wait()
    sums = lax.fori_loop(0, LANE // CHUNK, chunk, jnp.zeros((8, LANE), F32))
    if not full:
        return

    upright = jnp.concatenate(
        [down(place[1][:, n : n + LANE].astype(F32), LANE) for n in range(0, slots, LANE)], axis=0
    )
    away = upright - lax.broadcasted_iota(jnp.int32, (slots, LANE), 1).astype(F32)
    for block in range(STEPS * BAND):
        reads[:, block * LANE : (block + 1) * LANE] = jnp.where(
            away == float(block * LANE), 1.0, 0.0
        ).astype(BF16)
    y = fold(dot(reads[...], ys[...]))
    fetch_w.wait()
    z = w[...] * y
    z_out[0:slots, :] = z
    curve = jnp.sum((z * y).reshape(slots // 8, 8, LANE), axis=0)
    edge_out[...] = edges_of(place[1], jnp.concatenate(halves(z), axis=1))
    line = lax.broadcasted_iota(jnp.int32, (8, LANE), 0)
    one = jnp.sum(sums, axis=0, keepdims=True)
    two = jnp.sum(curve, axis=0, keepdims=True)
    z_out[slots : slots + 8, :] = jnp.where(line == 0, one, jnp.where(line == 1, two, 0.0))
    z_out[slots + 2 : slots + 4, :] = own[slots : slots + 2, :]


def turn_kernel(source, out):
    for lon in range(BAND):
        out[0, lon] = source[0, lon].T


def combine_kernel(*refs):
    *moments, scale, b, c0, c1, increment, residual, held, sems = refs
    total = moments[0][...]
    for part in moments[1:]:
        total = total + part[...]
    total = jnp.sum(total, axis=1, keepdims=True)
    base = total[2:3]
    m1 = total[3:4] / base
    m2 = total[0:1] / base
    m3 = total[1:2] / base
    eps = scale[0:1, 0:1]
    ap = 1.0 / (eps + m1)
    alpha = eps * ap
    beta = (m2 - m1 * m1) * ap * ap
    u = 1.0 + beta - alpha
    curve = eps * (u * u - 2.0 * u * ap * m1 + ap * ap * m2) + (
        u * u * m1 - 2.0 * u * ap * m2 + ap * ap * m3
    )
    a2p = beta / curve
    a2 = eps * a2p
    inc_b = alpha + a2 * u
    inc_c = -(a2 * ap)
    res_b = 1.0 - alpha - a2 * u
    res_c = a2 * ap - ap - a2p * u
    res_d = a2p * ap
    copies = []
    for f in range(b.shape[0]):
        for lon in range(BAND):
            b_now, c_now = b[f, lon], c0[f, lon]
            to = pl.ds(lon, LANE, stride=BAND)
            held[0, f, to, :] = inc_b * b_now + inc_c * c_now
            held[1, f, to, :] = res_b * b_now + res_c * c_now + res_d * c1[f, lon].T
        for n, target in enumerate((increment, residual)):
            copy = pltpu.make_async_copy(held.at[n, f], target.at[f], sems.at[n, f])
            copy.start()
            copies.append(copy)
    for copy in copies:
        copy.wait()


def params(mebibytes):
    return pltpu.CompilerParams(vmem_limit_bytes=mebibytes * 1024 * 1024)


def shards(
    obs_owner, obs_lonpos, obs_lat, obs_step, obs_top, innovation, obs_weight,
    wind_shift, wind_frac, vmix, hcoef,
):
    devices = lax.axis_size("lon")
    fields = vmix.shape[0]
    count = obs_owner.shape[0]
    cap = max(2, 2 * count // devices)
    slots = devices * cap
    shape = jax.ShapeDtypeStruct
    state = shape((fields, BAND, LANE, LANE), F32)
    rows = shape((slots, LANE), F32)
    edge = shape((2 * LANE, LANE), F32)
    small = shape((8, LANE), F32)
    more_rows = shape((slots + 8, LANE), F32)

    send = pl.pallas_call(
        pack_kernel,
        out_shape=shape((devices, 2 * cap + 8, LANE), F32),
        in_specs=[pl.BlockSpec(memory_space=pltpu.HBM)] * 7,
        scratch_shapes=[pltpu.VMEM((slots, LANE), F32)] * 2
        + [pltpu.VMEM((1, count), jnp.int32)] * 5
        + [pltpu.VMEM((LANE, count), F32)] * 2
        + [pltpu.SemaphoreType.DMA((7,))],
        compiler_params=params(60),
        name="pack",
    )(
        obs_owner.reshape(1, count), obs_lonpos.reshape(1, count), obs_lat.reshape(1, count),
        obs_step.reshape(1, count), obs_top.reshape(1, count), innovation, obs_weight,
    )
    mats, offs, fracs, scale = pl.pallas_call(
        prepare_kernel,
        out_shape=(
            shape((4, fields, 2 * LANE, 2 * LANE), BF16),
            shape((STEPS, LANE, LANE), F32),
            shape((STEPS, LANE, LANE), F32),
            small,
        ),
        compiler_params=params(44),
        name="prepare",
    )(wind_shift, wind_frac, vmix, hcoef)
    received = lax.all_to_all(send, "lon", split_axis=0, concat_axis=0, tiled=True)
    w, rows_d, edge_d = pl.pallas_call(
        unpack_kernel,
        out_shape=(rows, shape((slots + 8, LANE), F32), edge),
        compiler_params=params(44),
        name="unpack",
    )(received, scale)

    def along(value, hop):
        return lax.ppermute(value, "lon", [(i, (i + hop) % devices) for i in range(devices)])

    def swap(value, first):
        pairs = [((i + first) % devices, (i + 1 + first) % devices) for i in range(0, devices, 2)]
        return lax.ppermute(value, "lon", pairs + [(b, a) for a, b in pairs])

    def near(value):
        return swap(value, 0), value, swap(value, 1)

    def far(edges):
        return along(edges[LANE:], 2), along(edges[:LANE], -2)

    def scratch(full, size, batch, begin, end):
        wide = [b - a for a, b in regions(begin, end)]
        shapes = [
            pltpu.VMEM((3, STEPS * BAND * size, slots), BF16),
            pltpu.VMEM((3, LANE, slots), BF16),
            pltpu.VMEM((3, STEPS * BAND, 16, slots), BF16),
            pltpu.VMEM((3, slots, 2 * LANE), BF16),
            pltpu.VMEM((wide[0], size, LANE), F32),
            pltpu.VMEM((wide[1], size, LANE), F32),
            pltpu.VMEM((wide[2] * size, 2 * LANE), BF16),
            pltpu.VMEM((batch, wide[2], size, LANE), F32),
            pltpu.VMEM((batch, wide[1] * size, 2 * LANE), BF16),
            pltpu.VMEM((STEPS, LANE, LANE), F32),
            pltpu.SemaphoreType.DMA((2,)),
        ]
        if full:
            shapes.append(pltpu.VMEM((STEPS * BAND * LANE, 2 * LANE), BF16))
            shapes.append(pltpu.VMEM((slots, STEPS * BAND * LANE), BF16))
            shapes.append(pltpu.VMEM((fields, BAND * size, 2 * LANE), BF16))
            shapes.append(pltpu.VMEM((2, BAND, size, LANE), F32))
            shapes.append(pltpu.VMEM((slots, LANE), F32))
        return shapes

    def specs(count):
        return [pl.BlockSpec(memory_space=pltpu.SMEM)] + [
            pl.BlockSpec(memory_space=pltpu.VMEM)
        ] * count

    anywhere = pl.BlockSpec(memory_space=pl.ANY)

    def cost(columns):
        return pl.CostEstimate(
            flops=columns * fields * LANE * 8 * LANE * LANE,
            bytes_accessed=8 * 1024 * 1024,
            transcendentals=0,
        )

    odd = (lax.axis_index("lon") % 2).reshape(1)

    def sweep(rows_near, edges, facts, size, batch, behind):
        return pl.pallas_call(
            functools.partial(sweep_kernel, True, size, batch, -6, BAND + 3),
            out_shape=(state, more_rows, edge),
            in_specs=specs(10) + [anywhere] + specs(1)[1:] + [anywhere] * 2,
            scratch_shapes=scratch(True, size, batch, -6, BAND + 3),
            compiler_params=params(44),
            cost_estimate=cost(130),
            name="sweep",
        )(odd, *rows_near, *facts, *far(edges), mats, offs, fracs, hcoef, w, behind)

    block = pl.BlockSpec((1, BAND, LANE, LANE), lambda f: (f, 0, 0, 0))

    def turn(value):
        return pl.pallas_call(
            turn_kernel,
            out_shape=state,
            grid=(fields,),
            in_specs=[block],
            out_specs=block,
            compiler_params=params(44),
            cost_estimate=cost(8),
            name="turn",
        )(value)

    facts = near(rows_d)
    b, z0, edge0 = sweep(facts, edge_d, facts, 32, fields, scale)
    b = turn(b)
    c0, z1, _ = sweep(near(z0), edge0, facts, 32, fields, b)
    c0 = turn(c0)
    last = near(z1)
    c1 = pl.pallas_call(
        functools.partial(sweep_kernel, False, 32, fields, 0, BAND),
        out_shape=state,
        in_specs=specs(8) + [anywhere] + specs(1)[1:] + [anywhere],
        scratch_shapes=scratch(False, 32, fields, 0, BAND),
        compiler_params=params(44),
        cost_estimate=cost(60),
        name="last_sweep",
    )(odd, *last, *facts, mats, offs, fracs, hcoef, c0)

    single = z1[slots:]
    window = last[0][slots:] + single + last[2][slots:]
    covered, parts = 3, [window]
    while devices // covered > 1:
        window = functools.reduce(jnp.add, parts)
        count_of = min(devices // covered, 7)
        parts = [window] + [along(window, -k * covered) for k in range(1, count_of)]
        covered = covered * count_of
    parts = parts + [along(single, -(k - 1)) for k in range(covered, devices)]

    flat = shape((fields, LANE * BAND, LANE), F32)
    increment, residual = pl.pallas_call(
        combine_kernel,
        out_shape=(flat, flat),
        in_specs=[pl.BlockSpec(memory_space=pltpu.VMEM)] * (len(parts) + 4),
        out_specs=[pl.BlockSpec(memory_space=pl.ANY)] * 2,
        scratch_shapes=[
            pltpu.VMEM((2, fields, LANE * BAND, LANE), F32),
            pltpu.SemaphoreType.DMA((2, fields)),
        ],
        compiler_params=params(44),
        cost_estimate=cost(8),
        name="combine",
    )(*parts, scale, b, c0, c1)
    whole = (fields, LANE, BAND, LANE)
    return increment.reshape(whole), residual.reshape(whole)


def solution(mesh):
    profile = P(("member", "lon"))
    field = P("member", None, "lon", None)
    return jax.shard_map(
        shards,
        mesh=mesh,
        in_specs=(P("lon", "member"),) + (profile,) * 4 + (P("member", "lon"),) * 2 + (P(),) * 4,
        out_specs=(field, field),
        check_vma=False,
    )
```
